512 devices in a mesh: island: 8 (over y_lo, x), fsdp: 64 (over z, y_hi, core).
Axes of the slice: x: 4, y: 8 (y_hi: 4, y_lo: 2; y = y_hi * 2 + y_lo), z: 8, core: 2. Of those that a mesh axis runs over, the one named last changes fastest.
Arguments:
- tokens: bfloat16 [262144, 4096], P(('island', 'fsdp')), may hold values from -24 to 24
- target: bfloat16 [262144, 128], P(('island', 'fsdp')), may hold values from -6 to 6
- weight: float32 [8, 4096, 128], P('island', 'fsdp'), may hold values from -6 to 6
- gain: float32 [8, 4096], P('island', 'fsdp'), may hold values from 0.25 to 1.75
- first_weight: float32 [8, 4096, 128], P('island', 'fsdp'), may hold values from -6 to 6
- second_weight: float32 [8, 4096, 128], P('island', 'fsdp'), may hold values from 0.1 to 2
- first_gain: float32 [8, 4096], P('island', 'fsdp'), may hold values from -18 to 18
- second_gain: float32 [8, 4096], P('island', 'fsdp'), may hold values from 104857 to 2097152
- anchor: float32 [4096, 128], P('fsdp'), may hold values from -6 to 6
- snapshot: float32 [8, 4096, 128], P('island', 'fsdp'), may hold values from -6 to 6
- momentum: float32 [4096, 128], P('fsdp'), may hold values from -6 to 6
Outputs:
- values: bfloat16 [262144, 128], P(('island', 'fsdp'))
- weight_new: float32 [8, 4096, 128], P('island', 'fsdp')
- gain_new: float32 [8, 4096], P('island', 'fsdp')
- first_weight_new: float32 [8, 4096, 128], P('island', 'fsdp')
- second_weight_new: float32 [8, 4096, 128], P('island', 'fsdp')
- first_gain_new: float32 [8, 4096], P('island', 'fsdp')
- second_gain_new: float32 [8, 4096], P('island', 'fsdp')
- anchor_new: float32 [4096, 128], P('fsdp')
- momentum_new: float32 [4096, 128], P('fsdp')
The draws below stay inside these ranges and needn't reach their ends.
All inputs are finite; a program needn't handle non-finite values.
Results may differ from the reference program's by a relative error of at most 0.02.
Values may be sent and summed in bfloat16 or wider, within the bound.
A program may use at most 64 MiB of HBM per device.

```python
import math
import jax
import jax.numpy as jnp
from jax import lax

D = 4096
HEAD = 128
ISLANDS = 8
TOK_ISL = 32768
TOKENS = 262144


def with_spikes(entries, stream_key, source, target, shards_of, factor):
    def block_of(axis_at):
        return (jnp.arange(entries.shape[axis_at]) // (entries.shape[axis_at] // shards_of)).reshape((-1,) + (1,) * (entries.ndim - 1 - axis_at))

    first = jax.random.permutation(stream_key, shards_of)[block_of(target)]
    second = (block_of(target) + shards_of // 2) % shards_of
    return jnp.where((block_of(source) == first) | (block_of(source) == second), factor * entries, entries)


def levels(own_key, dims, cuts, low, largest):
    level = 1.0
    for position, shards_of in cuts:
        steps = jax.random.uniform(jax.random.fold_in(jax.random.fold_in(own_key, 6), position), (shards_of,), jnp.float32, low / len(cuts), largest / len(cuts))
        level = level * jnp.repeat(jnp.exp(steps), dims[position] // shards_of).reshape((-1,) + (1,) * (len(dims) - 1 - position))
    return level


def noise(rng, shape, scale, bound, cuts=(), kind=jnp.bfloat16):
    level = levels(rng, shape, cuts, -0.22, 0.18) if cuts else 1.0
    drawn = jax.random.normal(rng, shape, jnp.float32) * scale * level
    return jnp.minimum(jnp.maximum(drawn, -bound), bound).astype(kind)


def heavy_noise(key, dims, deviation, limit, split, heavy, held_as=jnp.bfloat16):
    result = deviation * jax.random.normal(key, dims, jnp.float32)
    if split:
        result = result * levels(key, dims, split, -0.22, 0.18)
    return jnp.clip(with_spikes(result, jax.random.fold_in(key, 3), *heavy), -limit, limit).astype(held_as)


def setup_inputs(seed: int = 0) -> dict:
    key_list = jax.random.split(jax.random.key(seed), 12)
    tokens = heavy_noise(key_list[0], (TOKENS, D), 1.0, 24.0, ((0, 512),), (0, 1, 512, 6.0))
    target = noise(key_list[1], (TOKENS, HEAD), 1.0, 6.0, ((0, 512),))
    weight = noise(key_list[2], (ISLANDS, D, HEAD), 1.0, 6.0, ((0, 8), (1, 64)), jnp.float32)
    gain = jnp.clip(1.0 + 0.15 * jax.random.normal(key_list[3], (ISLANDS, D), jnp.float32), 0.25, 1.75)
    first_weight = noise(key_list[4], (ISLANDS, D, HEAD), 1.0, 6.0, ((0, 8), (1, 64)), jnp.float32)
    second_weight = jnp.clip(jnp.exp(math.log(2.0) - 2.9957323 * jax.random.uniform(key_list[5], (ISLANDS, D, HEAD), jnp.float32) ** levels(key_list[5], (ISLANDS, D, HEAD), ((0, 8), (1, 64)), -0.2, 0.2)), 0.1, 2.0)
    first_gain = noise(key_list[6], (ISLANDS, D), 3.0, 18.0, ((0, 8), (1, 64)), jnp.float32)
    second_gain = jnp.clip(jnp.exp(math.log(2097152) - 2.995738 * jax.random.uniform(key_list[7], (ISLANDS, D), jnp.float32) ** levels(key_list[7], (ISLANDS, D), ((0, 8), (1, 64)), -0.2, 0.2)), 104857.0, 2097152)
    anchor = noise(key_list[8], (D, HEAD), 1.0, 6.0, ((0, 64),), jnp.float32)
    snapshot = noise(key_list[9], (ISLANDS, D, HEAD), 1.0, 6.0, ((0, 8), (1, 64)), jnp.float32)
    momentum = noise(key_list[10], (D, HEAD), 1.0, 6.0, ((0, 64),), jnp.float32)
    return {"tokens": tokens, "target": target, "weight": weight, "gain": gain, "first_weight": first_weight, "second_weight": second_weight, "first_gain": first_gain, "second_gain": second_gain, "anchor": anchor, "snapshot": snapshot, "momentum": momentum}


def adamw(param, grad, first, second):
    first_next = 0.9 * first + 0.1 * grad
    second_next = 0.95 * second + 0.05 * grad * grad
    inner = param - 0.01 * (first_next / (jnp.sqrt(second_next) + 1e-08) + 0.1 * param)
    return (inner, first_next, second_next)

def reference(tokens, target, weight, gain, first_weight, second_weight, first_gain, second_gain, anchor, snapshot, momentum):
    scale = 1.0 / float(D) ** 0.5
    values_list, weight_list, gain_list = ([], [], [])
    fw_list, sw_list, fg_list, sg_list, delta_list = ([], [], [], [], [])
    for island_idx in range(ISLANDS):
        rows_x = tokens[island_idx * TOK_ISL:(island_idx + 1) * TOK_ISL].astype(jnp.float32)
        rstd = 1.0 / jnp.sqrt(lax.optimization_barrier(jnp.mean(rows_x * rows_x, axis=1, keepdims=True)) + 1e-05)
        normed = (rows_x * rstd).astype(jnp.bfloat16)
        effective = (gain[island_idx][:, None] * weight[island_idx] * scale).astype(jnp.bfloat16)
        projected = jnp.dot(normed, effective, preferred_element_type=jnp.float32)
        values_list.append(projected.astype(jnp.bfloat16))
        target_rows = target[island_idx * TOK_ISL:(island_idx + 1) * TOK_ISL].astype(jnp.float32)
        error = (projected - target_rows).astype(jnp.bfloat16)
        summed = jnp.dot(normed.T, error, preferred_element_type=jnp.float32)
        grad_weight = gain[island_idx][:, None] * summed * scale
        grad_gain = lax.optimization_barrier(jnp.sum(weight[island_idx] * summed, axis=1)) * scale
        inner_w, fw, sw = adamw(weight[island_idx], grad_weight, first_weight[island_idx], second_weight[island_idx])
        inner_g, fg, sg = adamw(gain[island_idx], grad_gain, first_gain[island_idx], second_gain[island_idx])
        weight_list.append(inner_w)
        gain_list.append(inner_g)
        fw_list.append(fw)
        sw_list.append(sw)
        fg_list.append(fg)
        sg_list.append(sg)
        delta_list.append((anchor - snapshot[island_idx]).astype(jnp.bfloat16).astype(jnp.float32))
    total = delta_list[0]
    for more in delta_list[1:]:
        total = total + more
    mean_delta = total / ISLANDS
    momentum_new = 0.9 * momentum + mean_delta
    anchor_new = anchor - 0.7 * (mean_delta + 0.9 * momentum_new)
    weight_new = jnp.stack([0.5 * inner + 0.5 * anchor_new for inner in weight_list])
    return (jnp.concatenate(values_list, axis=0), weight_new, jnp.stack(gain_list), jnp.stack(fw_list), jnp.stack(sw_list), jnp.stack(fg_list), jnp.stack(sg_list), anchor_new, momentum_new)
```

```python
import functools

import jax
import jax.numpy as jnp
from jax import lax
from jax.experimental import pallas as pl
from jax.experimental.pallas import tpu as pltpu
from jax.sharding import PartitionSpec as P

MESH = pl.DeviceIdType.MESH
NZ, NY, NC = 8, 4, 2
F32, BF16 = jnp.float32, jnp.bfloat16


def ring_order(n):
    return sorted(range(1, n), key=lambda d: (min(d, n - d), d))


def adamw(param, grad, first, second):
    first_next = 0.9 * first + 0.1 * grad
    second_next = 0.95 * second + 0.05 * grad * grad
    inner = param - 0.01 * (first_next / (jnp.sqrt(second_next) + 1e-08) + 0.1 * param)
    return inner, first_next, second_next


def kernel(
    nz,
    ny,
    ni,
    tokens_hbm,
    target_hbm,
    weight_hbm,
    gain_ref,
    first_w_hbm,
    second_w_hbm,
    first_g_ref,
    second_g_ref,
    anchor_hbm,
    snapshot_hbm,
    momentum_hbm,
    values_ref,
    weight_new_ref,
    gain_new_ref,
    first_w_ref,
    second_w_ref,
    first_g_out,
    second_g_out,
    anchor_new_ref,
    momentum_new_ref,
    tok,
    tok_t,
    target,
    weight,
    first_w,
    second_w,
    anchor,
    snapshot,
    momentum,
    own,
    eff,
    squares,
    acc,
    err,
    delta,
    mine,
    give,
    take,
    part,
    recv_a,
    recv_b,
    sum_a,
    sum_b,
    send_a,
    send_b,
    last_a,
    last_b,
    summed,
    load_sem,
    tok_sem,
    send_sem,
    sib_sem,
    y_a_sem,
    z_b_sem,
    a_sem,
    b_sem,
    delta_sem,
    pair_sem,
    ra_sem,
    rb_sem,
    la_sem,
    lb_sem,
):
    f = lax.axis_index("fsdp")
    isl = lax.axis_index("island")
    z, y, c = f // (ny * NC), (f // NC) % ny, f % NC
    rows, head = own.shape
    half = rows // 2
    tall = tok.shape[0]
    width = ny * NC * rows
    dim = tok.shape[1]
    up, low = pl.ds(0, half), pl.ds(half, half)
    near_z, near_y = ring_order(nz), ring_order(ny)
    far_z, far_y = near_z[::-1], near_y[::-1]

    def at_z(d):
        return lax.rem(z + d, nz)

    def at_y(d):
        return lax.rem(y + d, ny)

    def to_z(d):
        return {"island": isl, "fsdp": (at_z(d) * ny + y) * NC + c}

    def to_y(d):
        return {"island": isl, "fsdp": (z * ny + at_y(d)) * NC + c}

    sibling = {"island": isl, "fsdp": (z * ny + y) * NC + 1 - c}

    def to_isl(d):
        return {"island": lax.rem(isl + d, ni), "fsdp": f}

    barrier = pltpu.get_barrier_semaphore()
    partners = [to_z(d) for d in far_z] + [to_y(d) for d in far_y] + [to_isl(d) for d in range(1, ni)] + [sibling]
    for partner in partners:
        pl.semaphore_signal(barrier, inc=1, device_id=partner, device_id_type=MESH)

    loads = [
        pltpu.make_async_copy(src, dst, load_sem.at[n])
        for n, (src, dst) in enumerate(
            [
                (weight_hbm.at[0], weight),
                (anchor_hbm, anchor),
                (snapshot_hbm.at[0], snapshot),
                (target_hbm, target),
                (first_w_hbm.at[0], first_w),
                (second_w_hbm.at[0], second_w),
                (momentum_hbm, momentum),
            ]
        )
    ]
    loads[0].start()
    for k in range(nz):
        cols = pl.ds(k * width, width)
        pltpu.make_async_copy(tokens_hbm.at[:, cols], tok.at[:, cols], tok_sem.at[k]).start()
    for load in loads[1:]:
        load.start()

    eye = lax.broadcasted_iota(jnp.int32, (rows, rows), 0) == lax.broadcasted_iota(jnp.int32, (rows, rows), 1)

    def as_column(row):
        return jnp.sum(jnp.where(eye, jnp.broadcast_to(row, (rows, rows)), 0.0), axis=1, keepdims=True)

    def as_row(column):
        return jnp.sum(jnp.where(eye, jnp.broadcast_to(column, (rows, rows)), 0.0), axis=0, keepdims=True)

    scale = 1.0 / float(dim) ** 0.5
    gain = as_column(gain_ref[...])
    loads[0].wait()
    own[...] = (gain * weight[...] * scale).astype(BF16)
    eff[z, y, c] = own[...]
    squares[...] = jnp.zeros_like(squares)

    def prepare(k, carry):
        cols = pl.ds(pl.multiple_of(k * width, width), width)
        pltpu.make_async_copy(tokens_hbm.at[:, cols], tok.at[:, cols], tok_sem.at[k]).wait()
        x = tok[:, cols]
        tok_t[cols, :] = x.T
        wide = x.astype(F32)
        total = squares[...]
        for j in range(width // head):
            piece = wide[:, j * head : (j + 1) * head]
            total = total + piece * piece
        squares[...] = total
        return carry

    lax.fori_loop(0, nz // 2, prepare, 0)

    sent = []

    def send(src, dst, sem, device):
        copy = pltpu.make_async_remote_copy(
            src_ref=src,
            dst_ref=dst,
            send_sem=send_sem.at[len(sent)],
            recv_sem=sem,
            device_id=device,
            device_id_type=MESH,
        )
        copy.start()
        sent.append(copy)

    def arrived(ref, sem):
        pltpu.make_async_copy(ref, ref, sem).wait()

    pl.semaphore_wait(barrier, len(partners))

    mine_up, mine_low = eff.at[z, y, c, up], eff.at[z, y, c, low]
    for d in far_y:
        send(own.at[up], mine_up, y_a_sem.at[y], to_y(d))
    for d in far_z:
        send(own.at[low], mine_low, z_b_sem.at[z], to_z(d))
    for d in far_z:
        send(own.at[up], mine_up, a_sem.at[z], to_z(d))
    for d in far_y:
        send(own.at[low], mine_low, b_sem.at[z], to_y(d))

    lax.fori_loop(nz // 2, nz, prepare, 0)

    def pass_up(d):
        block = eff.at[z, at_y(d), c, up]
        arrived(block, y_a_sem.at[at_y(d)])
        for e in far_z:
            send(block, block, a_sem.at[z], to_z(e))

    def pass_low(d):
        block = eff.at[at_z(d), y, c, low]
        arrived(block, z_b_sem.at[at_z(d)])
        for e in far_y:
            send(block, block, b_sem.at[at_z(d)], to_y(e))

    y_left, z_left = list(near_y), list(near_z)
    while y_left or z_left:
        for _ in range(2):
            if z_left:
                pass_low(z_left.pop(0))
        if y_left:
            pass_up(y_left.pop(0))

    mean_sq = jnp.sum(squares[...], axis=1, keepdims=True) / float(dim)
    rstd = lax.rsqrt(mean_sq + 1e-05)

    order = [0] + near_z

    def hand_over(n):
        zb = at_z(order[n])
        if n:
            arrived(eff.at[zb, :, c, up], a_sem.at[zb])
        arrived(eff.at[zb, pl.ds(0, ny - 1), c, low], b_sem.at[zb])
        block = eff.at[zb, :, c]
        send(block, block, sib_sem.at[n], sibling)

    def multiply(n):
        zb = at_z(order[n])
        arrived(eff.at[zb, :, 1 - c], sib_sem.at[n])
        cols = pl.ds(pl.multiple_of(zb * width, width), width)
        product = jnp.dot(tok[:, cols], eff[zb].reshape(width, head), preferred_element_type=F32)
        if n:
            acc[...] += product
        else:
            acc[...] = product

    for n in range(nz):
        hand_over(n)
        if n:
            multiply(n - 1)
    multiply(nz - 1)

    loads[3].wait()
    projected = acc[...] * rstd
    values_ref[...] = projected.astype(BF16)
    err[...] = ((projected - target[...].astype(F32)) * rstd).astype(BF16)

    back = far_z + [0]

    def terms(n):
        zb = at_z(back[n])
        cols = pl.ds(pl.multiple_of(zb * width, width), width)
        block = jnp.dot(tok_t[cols, :], err[...], preferred_element_type=F32).reshape(ny, NC, rows, head)
        first, second = block[:, 0], block[:, 1]
        mine[n] = jnp.where(c == 0, first, second)
        give[n] = jnp.where(c == 0, second, first).astype(BF16)
        send(give.at[n], take.at[n], pair_sem.at[n], sibling)

    def add_pair(n):
        arrived(take.at[n], pair_sem.at[n])
        part[n] = (mine[n] + take[n].astype(F32)).astype(BF16)
        if back[n]:
            send(part.at[n, :, up], recv_a.at[z], ra_sem.at[z], to_z(back[n]))

    group = nz // 2

    def send_low(g):
        span = pl.ds(g * group, group)
        for d in far_y:
            send(part.at[span, at_y(d), low], recv_b.at[y, span], rb_sem.at[g, y], to_y(d))

    lag = 2
    for n in range(nz + lag):
        if n < nz:
            terms(n)
        if n >= lag:
            add_pair(n - lag)
            if (n - lag + 1) % group == 0:
                send_low((n - lag) // group)

    loads[1].wait()
    loads[2].wait()
    delta[isl] = (anchor[...] - snapshot[...]).astype(BF16)
    for d in range(1, ni):
        send(delta.at[isl], delta.at[isl], delta_sem.at[isl], to_isl(d))

    def low_sums(g):
        span = pl.ds(g * group, group)
        total = part[span, y, low].astype(F32)
        for d in near_y:
            arrived(recv_b.at[at_y(d), span], rb_sem.at[g, at_y(d)])
            total = total + recv_b[at_y(d), span].astype(F32)
        sum_b[span] = total
        send_b[span] = total.astype(BF16)
        for n in range(g * group, (g + 1) * group):
            if back[n]:
                send(send_b.at[n], last_b.at[z], lb_sem.at[z], to_z(back[n]))

    low_sums(0)
    total = part[nz - 1, :, up].astype(F32)
    for d in near_z:
        arrived(recv_a.at[at_z(d)], ra_sem.at[at_z(d)])
        total = total + recv_a[at_z(d)].astype(F32)
    sum_a[...] = total
    send_a[...] = total.astype(BF16)
    for d in far_y:
        send(send_a.at[at_y(d)], last_a.at[y], la_sem.at[y], to_y(d))
    low_sums(1)

    loads[6].wait()
    for d in range(1, ni):
        there = lax.rem(isl + d, ni)
        arrived(delta.at[there], delta_sem.at[there])
    delta_sum = delta[0].astype(F32)
    for n in range(1, ni):
        delta_sum = delta_sum + delta[n].astype(F32)
    mean_delta = delta_sum / float(ni)
    momentum_next = 0.9 * momentum[...] + mean_delta
    anchor_next = anchor[...] - 0.7 * (mean_delta + 0.9 * momentum_next)
    momentum_new_ref[...] = momentum_next
    anchor_new_ref[...] = anchor_next

    total = sum_a[y]
    for d in near_y:
        arrived(last_a.at[at_y(d)], la_sem.at[at_y(d)])
        total = total + last_a[at_y(d)].astype(F32)
    summed[up, :] = total
    total = sum_b[nz - 1]
    for d in near_z:
        arrived(last_b.at[at_z(d)], lb_sem.at[at_z(d)])
        total = total + last_b[at_z(d)].astype(F32)
    summed[low, :] = total

    loads[4].wait()
    loads[5].wait()
    grad = summed[...]
    grad_gain = as_row(jnp.sum(weight[...] * grad, axis=1, keepdims=True)) * scale
    inner, first_next, second_next = adamw(weight[...], gain * grad * scale, first_w[...], second_w[...])
    weight_new_ref[0] = 0.5 * inner + 0.5 * anchor_next
    first_w_ref[0] = first_next
    second_w_ref[0] = second_next
    inner, first_next, second_next = adamw(gain_ref[...], grad_gain, first_g_ref[...], second_g_ref[...])
    gain_new_ref[...] = inner
    first_g_out[...] = first_next
    second_g_out[...] = second_next
    for copy in sent:
        copy.wait_send()


def per_device(nz, ny, ni, *args):
    tokens, target, weight = args[:3]
    tall, dim = tokens.shape
    _, rows, head = weight.shape
    half = rows // 2
    vmem = pl.BlockSpec(memory_space=pltpu.VMEM)
    hbm = pl.BlockSpec(memory_space=pl.ANY)
    shard, line = (1, rows, head), (1, rows)
    outs = [
        ((tall, head), BF16),
        (shard, F32),
        (line, F32),
        (shard, F32),
        (shard, F32),
        (line, F32),
        (line, F32),
        ((rows, head), F32),
        ((rows, head), F32),
    ]
    dma = pltpu.SemaphoreType.DMA
    sends = 2 * (nz - 1 + ny - 1) + 2 * (nz - 1) * (ny - 1) + nz
    sends += nz + (nz - 1) + 2 * (ny - 1) + (ni - 1) + (nz - 1) + (ny - 1)
    blocks = (nz, ny, rows, head)
    scratch = [
        pltpu.VMEM((tall, dim), BF16),
        pltpu.VMEM((dim, tall), BF16),
        pltpu.VMEM((tall, head), BF16),
        *[pltpu.VMEM((rows, head), F32) for _ in range(6)],
        pltpu.VMEM((rows, head), BF16),
        pltpu.VMEM((nz, ny, NC, rows, head), BF16),
        pltpu.VMEM((tall, head), F32),
        pltpu.VMEM((tall, head), F32),
        pltpu.VMEM((tall, head), BF16),
        pltpu.VMEM((ni, rows, head), BF16),
        pltpu.VMEM(blocks, F32),
        pltpu.VMEM(blocks, BF16),
        pltpu.VMEM(blocks, BF16),
        pltpu.VMEM(blocks, BF16),
        pltpu.VMEM((nz, ny, half, head), BF16),
        pltpu.VMEM((ny, nz, half, head), BF16),
        pltpu.VMEM((ny, half, head), F32),
        pltpu.VMEM((nz, half, head), F32),
        pltpu.VMEM((ny, half, head), BF16),
        pltpu.VMEM((nz, half, head), BF16),
        pltpu.VMEM((ny, half, head), BF16),
        pltpu.VMEM((nz, half, head), BF16),
        pltpu.VMEM((rows, head), F32),
        dma((7,)),
        dma((nz,)),
        dma((sends,)),
        dma((nz,)),
        dma((ny,)),
        dma((nz,)),
        dma((nz,)),
        dma((nz,)),
        dma((ni,)),
        dma((nz,)),
        dma((nz,)),
        dma((2, ny)),
        dma((ny,)),
        dma((nz,)),
    ]
    return pl.pallas_call(
        functools.partial(kernel, nz, ny, ni),
        out_shape=[jax.ShapeDtypeStruct(s, t) for s, t in outs],
        in_specs=[hbm, hbm, hbm, vmem, hbm, hbm, vmem, vmem, hbm, hbm, hbm],
        out_specs=[vmem] * len(outs),
        scratch_shapes=scratch,
        compiler_params=pltpu.CompilerParams(
            collective_id=0, has_side_effects=True, vmem_limit_bytes=40 * 2**20
        ),
        name="diloco_step",
    )(*args)


def solution(mesh, nz=NZ, ny=NY):
    rows = P(("island", "fsdp"), None)
    shard = P("island", "fsdp", None)
    line = P("island", "fsdp")
    whole = P("fsdp", None)
    return jax.shard_map(
        functools.partial(per_device, nz, ny, mesh.shape["island"]),
        mesh=mesh,
        in_specs=(rows, rows, shard, line, shard, shard, line, line, whole, shard, whole),
        out_specs=(rows, shard, line, shard, shard, line, line, whole, whole),
        check_vma=False,
    )
```

```python
import functools

import jax
import jax.numpy as jnp
from jax import lax
from jax.experimental import pallas as pl
from jax.experimental.pallas import tpu as pltpu
from jax.sharding import PartitionSpec as P

MESH = pl.DeviceIdType.MESH
NZ, NY, NC = 8, 4, 2
F32, BF16 = jnp.float32, jnp.bfloat16
PREPARED = {1: 5, 2: 7, 3: 8}


def ring_order(n):
    return sorted(range(1, n), key=lambda d: (min(d, n - d), d))


def adamw(param, grad, first, second):
    first_next = 0.9 * first + 0.1 * grad
    second_next = 0.95 * second + 0.05 * grad * grad
    inner = param - 0.01 * (first_next / (jnp.sqrt(second_next) + 1e-08) + 0.1 * param)
    return inner, first_next, second_next


def eye(n):
    return lax.broadcasted_iota(jnp.int32, (n, n), 0) == lax.broadcasted_iota(jnp.int32, (n, n), 1)


def as_column(row):
    n = row.shape[1]
    return jnp.sum(jnp.where(eye(n), jnp.broadcast_to(row, (n, n)), 0.0), axis=1, keepdims=True)


def as_row(column):
    n = column.shape[0]
    return jnp.sum(jnp.where(eye(n), jnp.broadcast_to(column, (n, n)), 0.0), axis=0, keepdims=True)


def exchange(
    nz,
    ny,
    ni,
    tokens_hbm,
    target_hbm,
    weight_hbm,
    gain_hbm,
    anchor_hbm,
    snapshot_hbm,
    momentum_hbm,
    values_ref,
    summed,
    anchor_new_ref,
    momentum_new_ref,
    tok,
    tok_t,
    target,
    weight,
    anchor,
    snapshot,
    momentum,
    gain_row,
    own,
    eff,
    squares,
    acc,
    err,
    delta,
    mine,
    give,
    take,
    part,
    recv_a,
    recv_b,
    send_a,
    send_b,
    last_a,
    last_b,
    load_sem,
    tok_sem,
    send_sem,
    sib_sem,
    y_a_sem,
    z_b_sem,
    a_sem,
    b_sem,
    delta_sem,
    pair_sem,
    ra_sem,
    rb_sem,
    la_sem,
    lb_sem,
):
    f = lax.axis_index("fsdp")
    isl = lax.axis_index("island")
    z, y, c = f // (ny * NC), (f // NC) % ny, f % NC
    rows, head = own.shape
    half = rows // 2
    tall = tok.shape[0]
    width = ny * NC * rows
    dim = tok.shape[1]
    up, low = pl.ds(0, half), pl.ds(half, half)
    near_z, near_y = ring_order(nz), ring_order(ny)
    far_z = near_z[::-1]

    def at_z(d):
        return lax.rem(z + d, nz)

    def at_y(d):
        return lax.rem(y + d, ny)

    def to_z(d):
        return {"island": isl, "fsdp": (at_z(d) * ny + y) * NC + c}

    def to_y(d):
        return {"island": isl, "fsdp": (z * ny + at_y(d)) * NC + c}

    sibling = {"island": isl, "fsdp": (z * ny + y) * NC + 1 - c}

    def to_isl(d):
        return {"island": lax.rem(isl + d, ni), "fsdp": f}

    barrier = pltpu.get_barrier_semaphore()
    partners = [to_z(d) for d in far_z] + [to_y(d) for d in near_y] + [to_isl(d) for d in range(1, ni)] + [sibling]
    for partner in partners:
        pl.semaphore_signal(barrier, inc=1, device_id=partner, device_id_type=MESH)

    loads = [
        pltpu.make_async_copy(src, dst, load_sem.at[n])
        for n, (src, dst) in enumerate(
            [
                (weight_hbm.at[0], weight),
                (anchor_hbm, anchor),
                (snapshot_hbm.at[0], snapshot),
                (target_hbm, target),
                (momentum_hbm, momentum),
                (gain_hbm, gain_row),
            ]
        )
    ]
    loads[5].start()
    loads[0].start()
    for k in range(nz):
        cols = pl.ds(k * width, width)
        pltpu.make_async_copy(tokens_hbm.at[:, cols], tok.at[:, cols], tok_sem.at[k]).start()
    for load in loads[1:5]:
        load.start()

    scale = 1.0 / float(dim) ** 0.5
    loads[5].wait()
    gain = as_column(gain_row[...])
    loads[0].wait()
    own[...] = (gain * weight[...] * scale).astype(BF16)
    eff[z, y, c] = own[...]
    squares[...] = jnp.zeros_like(squares)

    def prepare(k, carry):
        cols = pl.ds(pl.multiple_of(k * width, width), width)
        pltpu.make_async_copy(tokens_hbm.at[:, cols], tok.at[:, cols], tok_sem.at[k]).wait()
        x = tok[:, cols]
        tok_t[k] = x.T.reshape(ny, NC, 2, half, tall)
        wide = x.astype(F32)
        total = squares[...]
        for j in range(width // head):
            piece = wide[:, j * head : (j + 1) * head]
            total = total + piece * piece
        squares[...] = total
        return carry

    sent = []

    def send(src, dst, sem, device):
        copy = pltpu.make_async_remote_copy(
            src_ref=src,
            dst_ref=dst,
            send_sem=send_sem.at[len(sent)],
            recv_sem=sem,
            device_id=device,
            device_id_type=MESH,
        )
        copy.start()
        sent.append(copy)

    def arrived(ref, sem):
        pltpu.make_async_copy(ref, ref, sem).wait()

    pl.semaphore_wait(barrier, len(partners))

    mine_up, mine_low = eff.at[z, y, c, up], eff.at[z, y, c, low]
    for d in near_z:
        send(own.at[low], mine_low, z_b_sem.at[z], to_z(d))
    for d in near_y:
        send(own.at[up], mine_up, y_a_sem.at[y], to_y(d))

    def pass_up(d):
        block = eff.at[z, at_y(d), c, up]
        arrived(block, y_a_sem.at[at_y(d)])
        for e in near_z:
            send(block, block, a_sem.at[z], to_z(e))

    def pass_low(d):
        block = eff.at[at_z(d), y, c, low]
        arrived(block, z_b_sem.at[at_z(d)])
        for e in near_y:
            send(block, block, b_sem.at[at_z(d)], to_y(e))

    for d in near_z:
        send(own.at[up], mine_up, a_sem.at[z], to_z(d))
    for d in near_y:
        send(own.at[low], mine_low, b_sem.at[z], to_y(d))

    hops = [(min(d, nz - d), pass_low, d) for d in near_z] + [(2 * min(d, ny - d), pass_up, d) for d in near_y]
    hops.sort(key=lambda step: step[0])
    ready = 0
    for links, step, d in hops:
        if links in PREPARED and ready < min(PREPARED[links], nz):
            lax.fori_loop(ready, min(PREPARED[links], nz), prepare, 0)
            ready = min(PREPARED[links], nz)
        step(d)
    lax.fori_loop(ready, nz, prepare, 0)

    mean_sq = jnp.sum(squares[...], axis=1, keepdims=True) / float(dim)
    rstd = lax.rsqrt(mean_sq + 1e-05)

    order = [0] + near_z

    def hand_over(n):
        zb = at_z(order[n])
        if n:
            arrived(eff.at[zb, :, c, up], a_sem.at[zb])
        arrived(eff.at[zb, pl.ds(0, ny - 1), c, low], b_sem.at[zb])
        block = eff.at[zb, :, c]
        send(block, block, sib_sem.at[n], sibling)

    def multiply(n):
        zb = at_z(order[n])
        arrived(eff.at[zb, :, 1 - c], sib_sem.at[n])
        cols = pl.ds(pl.multiple_of(zb * width, width), width)
        product = jnp.dot(tok[:, cols], eff[zb].reshape(width, head), preferred_element_type=F32)
        if n:
            acc[...] += product
        else:
            acc[...] = product

    for n in range(nz):
        hand_over(n)
        if n:
            multiply(n - 1)
    multiply(nz - 1)

    loads[3].wait()
    projected = acc[...] * rstd
    values_ref[...] = projected.astype(BF16)
    err[...] = ((projected - target[...].astype(F32)) * rstd).astype(BF16)

    back_y, back_z = near_y[::-1] + [0], far_z + [0]
    pairs = [back_z[n : n + 2] for n in range(0, nz, 2)]
    groups = [g for up_down in zip(range(ny), range(ny)) for g in (("up", up_down[0]), ("low", up_down[1]))]

    def product(lhs):
        return jnp.dot(lhs, err[...], preferred_element_type=F32).reshape(-1, NC, half, head)

    def terms(g):
        kind, n = groups[g]
        if kind == "up":
            block = product(tok_t[:, at_y(back_y[n]), :, 0].reshape(nz * NC * half, tall))
            first, second = block[:, 0], block[:, 1]
            mine[g] = jnp.where(c == 0, first, second)
            give[g] = jnp.where(c == 0, second, first).astype(BF16)
        else:
            for m, d in enumerate(pairs[n]):
                block = product(tok_t[at_z(d), :, :, 1].reshape(ny * NC * half, tall))
                first, second = block[:, 0], block[:, 1]
                rows_m = pl.ds(m * ny, ny)
                mine[g, rows_m] = jnp.where(c == 0, first, second)
                give[g, rows_m] = jnp.where(c == 0, second, first).astype(BF16)
        send(give.at[g], take.at[g], pair_sem.at[g], sibling)

    def add_pair(g):
        kind, n = groups[g]
        arrived(take.at[g], pair_sem.at[g])
        part[g] = (mine[g] + take[g].astype(F32)).astype(BF16)
        if kind == "up":
            for d in near_z:
                send(part.at[g, at_z(d)], recv_a.at[n, d - 1], ra_sem.at[n], to_z(d))
        else:
            for d in near_y:
                for m in range(2):
                    send(part.at[g, m * ny + at_y(d)], recv_b.at[n, d - 1, m], rb_sem.at[n], to_y(d))

    lag = 2
    for g in range(len(groups) + lag):
        if g < len(groups):
            terms(g)
        if g >= lag:
            add_pair(g - lag)

    loads[1].wait()
    loads[2].wait()
    delta[isl] = (anchor[...] - snapshot[...]).astype(BF16)
    for d in range(1, ni):
        send(delta.at[isl], delta.at[isl], delta_sem.at[isl], to_isl(d))

    kept = {}

    def add_up(g, n):
        arrived(recv_a.at[n], ra_sem.at[n])
        total = part[g, z].astype(F32) + jnp.sum(recv_a[n].astype(F32), axis=0)
        d = back_y[n]
        if d:
            send_a[n] = total.astype(BF16)
            send(send_a.at[n], last_a.at[d - 1], la_sem.at[0], to_y(d))
        else:
            kept["up"] = total

    def add_low(g, n):
        arrived(recv_b.at[n], rb_sem.at[n])
        for m, d in enumerate(pairs[n]):
            total = part[g, m * ny + y].astype(F32)
            for e in range(ny - 1):
                total = total + recv_b[n, e, m].astype(F32)
            if d:
                send_b[d - 1] = total.astype(BF16)
                send(send_b.at[d - 1], last_b.at[d - 1], lb_sem.at[0], to_z(d))
            else:
                kept["low"] = total

    for g, (kind, n) in enumerate(groups):
        if kind == "low":
            add_low(g, n)
        elif back_y[n]:
            add_up(g, n)
    add_up(len(groups) - 2, ny - 1)

    loads[4].wait()
    for d in range(1, ni):
        there = lax.rem(isl + d, ni)
        arrived(delta.at[there], delta_sem.at[there])
    delta_sum = delta[0].astype(F32)
    for n in range(1, ni):
        delta_sum = delta_sum + delta[n].astype(F32)
    mean_delta = delta_sum / float(ni)
    momentum_next = 0.9 * momentum[...] + mean_delta
    anchor_next = anchor[...] - 0.7 * (mean_delta + 0.9 * momentum_next)
    momentum_new_ref[...] = momentum_next
    anchor_new_ref[...] = anchor_next

    arrived(last_a, la_sem.at[0])
    summed[up, :] = kept["up"] + jnp.sum(last_a[...].astype(F32), axis=0)
    arrived(last_b, lb_sem.at[0])
    summed[low, :] = kept["low"] + jnp.sum(last_b[...].astype(F32), axis=0)
    for copy in sent:
        copy.wait_send()


def finish(
    dim,
    values,
    summed,
    anchor_new,
    momentum_new,
    weight,
    gain,
    first_w,
    second_w,
    first_g,
    second_g,
    values_out,
    weight_out,
    gain_out,
    first_w_out,
    second_w_out,
    first_g_out,
    second_g_out,
    anchor_out,
    momentum_out,
    weight_new,
    gain_new,
    first_w_new,
    second_w_new,
    first_g_new,
    second_g_new,
    sem,
):
    scale = 1.0 / float(dim) ** 0.5
    started = []

    def store(src, dst):
        copy = pltpu.make_async_copy(src, dst, sem.at[len(started)])
        copy.start()
        started.append(copy)

    store(values, values_out)
    store(anchor_new, anchor_out)
    store(momentum_new, momentum_out)
    grad = summed[...]
    old = weight[0]
    grad_weight = as_column(gain[...]) * grad * scale
    inner, first_w_new[0], second_w_new[0] = adamw(old, grad_weight, first_w[0], second_w[0])
    weight_new[0] = 0.5 * inner + 0.5 * anchor_new[...]
    store(weight_new, weight_out)
    store(first_w_new, first_w_out)
    store(second_w_new, second_w_out)
    grad_gain = as_row(jnp.sum(old * grad, axis=1, keepdims=True)) * scale
    gain_new[...], first_g_new[...], second_g_new[...] = adamw(gain[...], grad_gain, first_g[...], second_g[...])
    store(gain_new, gain_out)
    store(first_g_new, first_g_out)
    store(second_g_new, second_g_out)
    for copy in started:
        copy.wait()


def per_device(
    nz,
    ny,
    ni,
    tokens,
    target,
    weight,
    gain,
    first_weight,
    second_weight,
    first_gain,
    second_gain,
    anchor,
    snapshot,
    momentum,
):
    tall, dim = tokens.shape
    _, rows, head = weight.shape
    half = rows // 2
    vmem = pl.BlockSpec(memory_space=pltpu.VMEM)
    hbm = pl.BlockSpec(memory_space=pl.ANY)
    shard, line = (1, rows, head), (1, rows)
    whole = (rows, head)
    dma = pltpu.SemaphoreType.DMA
    sends = 2 * (nz - 1 + ny - 1) + 2 * (nz - 1) * (ny - 1) + nz
    sends += 2 * ny + ny * (nz - 1) + nz * (ny - 1) + (ni - 1) + (nz - 1) + (ny - 1)
    blocks = (2 * ny, nz, half, head)
    scratch = [
        pltpu.VMEM((tall, dim), BF16),
        pltpu.VMEM((nz, ny, NC, 2, half, tall), BF16),
        pltpu.VMEM((tall, head), BF16),
        *[pltpu.VMEM((rows, head), F32) for _ in range(4)],
        pltpu.VMEM(line, F32),
        pltpu.VMEM((rows, head), BF16),
        pltpu.VMEM((nz, ny, NC, rows, head), BF16),
        pltpu.VMEM((tall, head), F32),
        pltpu.VMEM((tall, head), F32),
        pltpu.VMEM((tall, head), BF16),
        pltpu.VMEM((ni, rows, head), BF16),
        pltpu.VMEM(blocks, F32),
        pltpu.VMEM(blocks, BF16),
        pltpu.VMEM(blocks, BF16),
        pltpu.VMEM(blocks, BF16),
        pltpu.VMEM((ny, nz - 1, half, head), BF16),
        pltpu.VMEM((ny, ny - 1, 2, half, head), BF16),
        pltpu.VMEM((ny - 1, half, head), BF16),
        pltpu.VMEM((nz - 1, half, head), BF16),
        pltpu.VMEM((ny - 1, half, head), BF16),
        pltpu.VMEM((nz - 1, half, head), BF16),
        dma((6,)),
        dma((nz,)),
        dma((sends,)),
        dma((nz,)),
        dma((ny,)),
        dma((nz,)),
        dma((nz,)),
        dma((nz,)),
        dma((ni,)),
        dma((2 * ny,)),
        dma((ny,)),
        dma((ny,)),
        dma((1,)),
        dma((1,)),
    ]

    def in_hbm(x):
        return pltpu.with_memory_space_constraint(x, pltpu.HBM)

    values, summed, anchor_new, momentum_new = pl.pallas_call(
        functools.partial(exchange, nz, ny, ni),
        out_shape=[
            pltpu.VMEM((tall, head), BF16),
            pltpu.VMEM(whole, F32),
            pltpu.VMEM(whole, F32),
            pltpu.VMEM(whole, F32),
        ],
        in_specs=[hbm] * 7,
        out_specs=[vmem] * 4,
        scratch_shapes=scratch,
        compiler_params=pltpu.CompilerParams(
            collective_id=0, has_side_effects=True, vmem_limit_bytes=24 * 2**20
        ),
        name="exchange",
    )(in_hbm(tokens), in_hbm(target), in_hbm(weight), in_hbm(gain), in_hbm(anchor), in_hbm(snapshot), in_hbm(momentum))
    shapes = [(tall, head), shard, line, shard, shard, line, line, whole, whole]
    return pl.pallas_call(
        functools.partial(finish, dim),
        out_shape=[pltpu.HBM(shape, F32 if n else BF16) for n, shape in enumerate(shapes)],
        in_specs=[vmem] * 10,
        out_specs=[hbm] * 9,
        scratch_shapes=[pltpu.VMEM(shape, F32) for shape in shapes[1:7]] + [dma((9,))],
        compiler_params=pltpu.CompilerParams(vmem_limit_bytes=8 * 2**20),
        name="finish",
    )(
        values,
        summed,
        anchor_new,
        momentum_new,
        weight,
        gain,
        first_weight,
        second_weight,
        first_gain,
        second_gain,
    )


def solution(mesh, nz=NZ, ny=NY):
    rows = P(("island", "fsdp"), None)
    shard = P("island", "fsdp", None)
    line = P("island", "fsdp")
    whole = P("fsdp", None)
    return jax.shard_map(
        functools.partial(per_device, nz, ny, mesh.shape["island"]),
        mesh=mesh,
        in_specs=(rows, rows, shard, line, shard, shard, line, line, whole, shard, whole),
        out_specs=(rows, shard, line, shard, shard, line, line, whole, whole),
        check_vma=False,
    )
```

```python
import functools

import jax
import jax.numpy as jnp
from jax import lax
from jax.experimental import pallas as pl
from jax.experimental.pallas import tpu as pltpu
from jax.sharding import PartitionSpec as P

MESH = pl.DeviceIdType.MESH
NZ, NY, NC = 8, 4, 2
F32, BF16 = jnp.float32, jnp.bfloat16


def ring_order(n):
    return sorted(range(1, n), key=lambda d: (min(d, n - d), d))


def spans(links, n):
    late = [links.count(1), sum(k < n // 2 for k in links), len(links)]
    cuts = [1] + sorted({1 + k for k in late})
    return list(zip(cuts[:-1], cuts[1:]))


def adamw(param, grad, first, second):
    first_next = 0.9 * first + 0.1 * grad
    second_next = 0.95 * second + 0.05 * grad * grad
    inner = param - 0.01 * (first_next / (jnp.sqrt(second_next) + 1e-08) + 0.1 * param)
    return inner, first_next, second_next


def eye(n):
    return lax.broadcasted_iota(jnp.int32, (n, n), 0) == lax.broadcasted_iota(jnp.int32, (n, n), 1)


def as_column(row):
    n = row.shape[1]
    return jnp.sum(jnp.where(eye(n), jnp.broadcast_to(row, (n, n)), 0.0), axis=1, keepdims=True)


def as_row(column):
    n = column.shape[0]
    return jnp.sum(jnp.where(eye(n), jnp.broadcast_to(column, (n, n)), 0.0), axis=0, keepdims=True)


def exchange(
    nz,
    ny,
    ni,
    tokens_hbm,
    target_hbm,
    weight_hbm,
    gain_hbm,
    anchor_hbm,
    snapshot_hbm,
    momentum_hbm,
    values_ref,
    summed,
    anchor_new_ref,
    momentum_new_ref,
    tok,
    halves,
    peer,
    target,
    target_t,
    weight,
    anchor,
    snapshot,
    momentum,
    gain_row,
    own,
    eff_a,
    eff_b,
    squares,
    acc,
    other,
    err_t,
    delta,
    part_a,
    part_b,
    recv_a,
    recv_b,
    send_a,
    send_b,
    last_a,
    last_b,
    load_sem,
    tok_sem,
    push_sem,
    peer_sem,
    send_sem,
    pair_sem,
    ya_sem,
    za_sem,
    zb_sem,
    yb_sem,
    delta_sem,
    ra_sem,
    rb_sem,
    la_sem,
    lb_sem,
):
    f = lax.axis_index("fsdp")
    isl = lax.axis_index("island")
    z, y, c = f // (ny * NC), (f // NC) % ny, f % NC
    rows, head = own.shape
    half = rows // 2
    tall = tok.shape[0]
    width = ny * NC * rows
    dim = tok.shape[1]
    up, low = pl.ds(0, half), pl.ds(half, half)
    near_z, near_y = ring_order(nz), ring_order(ny)
    back_z, back_y = near_z[::-1] + [0], near_y[::-1] + [0]
    place_z = {d: n for n, d in enumerate([0] + near_z)}
    hi, lo = y // 2, y % 2
    spans_z = spans([min(d, nz - d) for d in near_z], nz)
    spans_back_z = [(nz - stop, nz - max(start, 1)) for start, stop in spans_z[::-1]]
    spans_back_z[-1] = (spans_back_z[-1][0], nz)
    spans_back_y = [span for span in ((0, 1), (1, ny - 1), (ny - 1, ny)) if span[0] < span[1]]

    def at_z(d):
        return lax.rem(z + d, nz)

    def at_y(d):
        return lax.rem(y + d, ny)

    def to_z(d):
        return {"island": isl, "fsdp": (at_z(d) * ny + y) * NC + c}

    def to_y(d):
        return {"island": isl, "fsdp": (z * ny + at_y(d)) * NC + c}

    sibling = {"island": isl, "fsdp": (z * ny + y) * NC + 1 - c}

    def to_isl(d):
        return {"island": lax.rem(isl + d, ni), "fsdp": f}

    barrier = pltpu.get_barrier_semaphore()
    partners = [to_z(d) for d in near_z] + [to_y(d) for d in near_y] + [to_isl(d) for d in range(1, ni)] + [sibling]
    for partner in partners:
        pl.semaphore_signal(barrier, inc=1, device_id=partner, device_id_type=MESH)

    loads = [
        pltpu.make_async_copy(src, dst, load_sem.at[n])
        for n, (src, dst) in enumerate(
            [
                (weight_hbm.at[0], weight),
                (anchor_hbm, anchor),
                (snapshot_hbm.at[0], snapshot),
                (target_hbm, target.at[0]),
                (momentum_hbm, momentum),
                (gain_hbm, gain_row),
            ]
        )
    ]
    loads[5].start()
    loads[0].start()
    for k in range(nz):
        cols = pl.ds(k * width, width)
        pltpu.make_async_copy(tokens_hbm.at[:, cols], tok.at[:, cols], tok_sem.at[k]).start()
    for load in loads[1:5]:
        load.start()

    scale = 1.0 / float(dim) ** 0.5
    loads[5].wait()
    gain = as_column(gain_row[...])
    loads[0].wait()
    own[...] = (gain * weight[...] * scale).astype(BF16)
    eff_a[0, hi, lo] = own[up]
    eff_b[y, 0] = own[low]

    sent = []

    def send(src, dst, sem, device):
        copy = pltpu.make_async_remote_copy(
            src_ref=src,
            dst_ref=dst,
            send_sem=send_sem.at[len(sent)],
            recv_sem=sem,
            device_id=device,
            device_id_type=MESH,
        )
        copy.start()
        sent.append(copy)

    def arrived(ref, sem):
        pltpu.make_async_copy(ref, ref, sem).wait()

    pl.semaphore_wait(barrier, len(partners))

    for d in near_z:
        n = place_z[nz - d]
        send(own.at[low], eff_b.at[y, n], zb_sem.at[n], to_z(d))
    for d in near_y:
        send(own.at[up], eff_a.at[0, hi, lo], ya_sem.at[1 - d % 2], to_y(d))
    for d in near_z:
        send(own.at[up], eff_a.at[nz - d, hi, lo], za_sem.at[nz - d], to_z(d))
    for d in near_y:
        send(own.at[low], eff_b.at[y, 0], yb_sem.at[0], to_y(d))
    loads[3].wait()
    send(target.at[0], target.at[1], pair_sem.at[0], sibling)
    squares[0] = jnp.zeros((8, tall), F32)

    def push(k):
        return pltpu.make_async_remote_copy(
            src_ref=halves.at[k, 1 - c],
            dst_ref=peer.at[k],
            send_sem=push_sem.at[k],
            recv_sem=peer_sem.at[k],
            device_id=sibling,
            device_id_type=MESH,
        )

    def prepare(k, carry):
        cols = pl.ds(pl.multiple_of(k * width, width), width)
        pltpu.make_async_copy(tokens_hbm.at[:, cols], tok.at[:, cols], tok_sem.at[k]).wait()
        turned = tok[:, cols].T
        block = turned.reshape(ny, NC, rows, tall)
        for core in range(NC):
            halves[k, core] = block[:, core]
        push(k).start()
        wide = turned.astype(F32)
        squares[0] += jnp.sum((wide * wide).reshape(width // 8, 8, tall), axis=0)
        return carry

    def pass_low(g):
        start, stop = spans_z[g]
        for n in range(start, stop):
            arrived(eff_b.at[y, n], zb_sem.at[n])
        span = eff_b.at[y, pl.ds(start, stop - start)]
        for d in near_y:
            send(span, span, yb_sem.at[1 + g], to_y(d))

    def pass_up(other_parity):
        if other_parity:
            arrived(eff_a.at[0, :, 1 - lo], ya_sem.at[0])
        else:
            arrived(eff_a.at[0, 1 - hi, lo], ya_sem.at[1])
        for d in near_z:
            if other_parity:
                send(eff_a.at[0, :, 1 - lo], eff_a.at[nz - d, :, 1 - lo], za_sem.at[nz - d], to_z(d))
            else:
                send(eff_a.at[0, 1 - hi, lo], eff_a.at[nz - d, 1 - hi, lo], za_sem.at[nz - d], to_z(d))

    lax.fori_loop(0, nz // 2, prepare, 0)
    pass_low(0)
    lax.fori_loop(nz // 2, nz * 3 // 4, prepare, 0)
    pass_up(True)
    for g in range(1, len(spans_z) - 1):
        pass_low(g)
    if ny > 2:
        pass_up(False)
    pass_low(len(spans_z) - 1)
    lax.fori_loop(nz * 3 // 4, nz, prepare, 0)

    send(squares.at[0], squares.at[1], pair_sem.at[1], sibling)
    arrived(target.at[1], pair_sem.at[0])
    for n in range(2):
        target_t[n] = target[n].T
    arrived(squares.at[1], pair_sem.at[1])
    rstd = [lax.rsqrt(jnp.sum(squares[n], axis=0, keepdims=True) / float(dim) + 1e-05) for n in range(2)]

    for n, d in enumerate([0] + near_z):
        zb = at_z(d)
        if d:
            arrived(eff_a.at[d], za_sem.at[d])
        for g, (start, stop) in enumerate([(0, 1)] + spans_z):
            if n == start:
                arrived(eff_b.at[pl.ds(0, ny - 1), pl.ds(start, stop - start)], yb_sem.at[g])
        arrived(peer.at[zb], peer_sem.at[zb])
        upper = eff_a[d].reshape(ny, 1, half, head)
        block = jnp.concatenate([upper, eff_b[:, n][:, None]], axis=1).reshape(ny * rows, head)
        for m, side in enumerate((halves[zb, c], peer[zb])):
            partial = lax.dot_general(
                block, side.reshape(ny * rows, tall), (((0,), (0,)), ((), ())), preferred_element_type=F32
            )
            if n:
                acc[m] += partial
            else:
                acc[m] = partial
    for m in range(2):
        send(acc.at[m], other.at[1 - m], pair_sem.at[2 + m], sibling)

    def projected(m):
        return (acc[m] + other[m]) * rstd[m]

    for m in range(2):
        arrived(other.at[1 - m], pair_sem.at[2 + m])
    for m in range(2):
        err_t[m] = ((projected(m) - target_t[m].astype(F32)) * rstd[m]).astype(BF16)

    def product(left, right):
        total = None
        for m, side in enumerate((left, right)):
            term = lax.dot_general(
                side.reshape(-1, tall), err_t[m], (((1,), (1,)), ((), ())), preferred_element_type=F32
            )
            total = term if m == 0 else total + term
        return total.astype(BF16).reshape(-1, half, head)

    def terms_up(g):
        start, stop = spans_back_y[g]
        for n in range(start, stop):
            yb = at_y(back_y[n])
            part_a[:, n] = product(halves[:, c, yb, up], peer[:, yb, up])
        span = pl.ds(start, stop - start)
        for d in near_z:
            send(part_a.at[at_z(d), span], recv_a.at[d - 1, span], ra_sem.at[g], to_z(d))

    def terms_low(g):
        start, stop = spans_back_z[g]
        for n in range(start, stop):
            zb = at_z(back_z[n])
            part_b[:, n] = product(halves[zb, c, :, low], peer[zb, :, low])
        span = pl.ds(start, stop - start)
        for d in near_y:
            send(part_b.at[at_y(d), span], recv_b.at[d - 1, span], rb_sem.at[g], to_y(d))

    for g in range(3):
        if g < len(spans_back_z):
            terms_low(g)
        if g < len(spans_back_y):
            terms_up(g)

    loads[1].wait()
    loads[2].wait()
    delta[isl] = (anchor[...] - snapshot[...]).astype(BF16)
    for d in range(1, ni):
        send(delta.at[isl], delta.at[isl], delta_sem.at[isl], to_isl(d))

    values_ref[...] = projected(0).astype(BF16).T

    kept = {}

    def add_up(g):
        start, stop = spans_back_y[g]
        span = pl.ds(start, stop - start)
        arrived(recv_a.at[:, span], ra_sem.at[g])
        for n in range(start, stop):
            d = back_y[n]
            total = part_a[z, n].astype(F32) + jnp.sum(recv_a[:, n].astype(F32), axis=0)
            if d:
                send_a[n] = total.astype(BF16)
                send(send_a.at[n], last_a.at[d - 1], la_sem.at[0], to_y(d))
            else:
                kept["up"] = total

    def add_low(g):
        start, stop = spans_back_z[g]
        span = pl.ds(start, stop - start)
        arrived(recv_b.at[:, span], rb_sem.at[g])
        for n in range(start, stop):
            d = back_z[n]
            total = part_b[y, n].astype(F32) + jnp.sum(recv_b[:, n].astype(F32), axis=0)
            if d:
                send_b[d - 1] = total.astype(BF16)
                send(send_b.at[d - 1], last_b.at[d - 1], lb_sem.at[0], to_z(d))
            else:
                kept["low"] = total

    for g in range(3):
        if g < len(spans_back_z):
            add_low(g)
        if g < len(spans_back_y) - 1:
            add_up(g)
    add_up(len(spans_back_y) - 1)

    loads[4].wait()
    for d in range(1, ni):
        there = lax.rem(isl + d, ni)
        arrived(delta.at[there], delta_sem.at[there])
    delta_sum = delta[0].astype(F32)
    for n in range(1, ni):
        delta_sum = delta_sum + delta[n].astype(F32)
    mean_delta = delta_sum / float(ni)
    momentum_next = 0.9 * momentum[...] + mean_delta
    anchor_next = anchor[...] - 0.7 * (mean_delta + 0.9 * momentum_next)
    momentum_new_ref[...] = momentum_next
    anchor_new_ref[...] = anchor_next

    arrived(last_a, la_sem.at[0])
    summed[up, :] = kept["up"] + jnp.sum(last_a[...].astype(F32), axis=0)
    arrived(last_b, lb_sem.at[0])
    summed[low, :] = kept["low"] + jnp.sum(last_b[...].astype(F32), axis=0)
    for copy in sent:
        copy.wait_send()
    for k in range(nz):
        push(k).wait_send()


def finish(
    dim,
    values,
    summed,
    anchor_new,
    momentum_new,
    weight,
    gain,
    first_w,
    second_w,
    first_g,
    second_g,
    values_out,
    weight_out,
    gain_out,
    first_w_out,
    second_w_out,
    first_g_out,
    second_g_out,
    anchor_out,
    momentum_out,
    weight_new,
    gain_new,
    first_w_new,
    second_w_new,
    first_g_new,
    second_g_new,
    sem,
):
    scale = 1.0 / float(dim) ** 0.5
    started = []

    def store(src, dst):
        copy = pltpu.make_async_copy(src, dst, sem.at[len(started)])
        copy.start()
        started.append(copy)

    store(values, values_out)
    store(anchor_new, anchor_out)
    store(momentum_new, momentum_out)
    grad = summed[...]
    old = weight[0]
    grad_weight = as_column(gain[...]) * grad * scale
    inner, first_w_new[0], second_w_new[0] = adamw(old, grad_weight, first_w[0], second_w[0])
    weight_new[0] = 0.5 * inner + 0.5 * anchor_new[...]
    store(weight_new, weight_out)
    store(first_w_new, first_w_out)
    store(second_w_new, second_w_out)
    grad_gain = as_row(jnp.sum(old * grad, axis=1, keepdims=True)) * scale
    gain_new[...], first_g_new[...], second_g_new[...] = adamw(gain[...], grad_gain, first_g[...], second_g[...])
    store(gain_new, gain_out)
    store(first_g_new, first_g_out)
    store(second_g_new, second_g_out)
    for copy in started:
        copy.wait()


def per_device(
    nz,
    ny,
    ni,
    tokens,
    target,
    weight,
    gain,
    first_weight,
    second_weight,
    first_gain,
    second_gain,
    anchor,
    snapshot,
    momentum,
):
    tall, dim = tokens.shape
    _, rows, head = weight.shape
    half = rows // 2
    vmem = pl.BlockSpec(memory_space=pltpu.VMEM)
    hbm = pl.BlockSpec(memory_space=pl.ANY)
    shard, line = (1, rows, head), (1, rows)
    whole = (rows, head)
    dma = pltpu.SemaphoreType.DMA
    sends = 4 * (nz - 1) + 5 * (ny - 1) + 4
    sends += 4 * (nz - 1) + 4 * (ny - 1) + (ni - 1)
    scratch = [
        pltpu.VMEM((tall, dim), BF16),
        pltpu.VMEM((nz, NC, ny, rows, tall), BF16),
        pltpu.VMEM((nz, ny, rows, tall), BF16),
        pltpu.VMEM((2, tall, head), BF16),
        pltpu.VMEM((2, head, tall), BF16),
        *[pltpu.VMEM((rows, head), F32) for _ in range(4)],
        pltpu.VMEM(line, F32),
        pltpu.VMEM((rows, head), BF16),
        pltpu.VMEM((nz, ny // 2, 2, half, head), BF16),
        pltpu.VMEM((ny, nz, half, head), BF16),
        pltpu.VMEM((2, 8, tall), F32),
        pltpu.VMEM((2, head, tall), F32),
        pltpu.VMEM((2, head, tall), F32),
        pltpu.VMEM((2, head, tall), BF16),
        pltpu.VMEM((ni, rows, head), BF16),
        pltpu.VMEM((nz, ny, half, head), BF16),
        pltpu.VMEM((ny, nz, half, head), BF16),
        pltpu.VMEM((nz - 1, ny, half, head), BF16),
        pltpu.VMEM((ny - 1, nz, half, head), BF16),
        pltpu.VMEM((ny - 1, half, head), BF16),
        pltpu.VMEM((nz - 1, half, head), BF16),
        pltpu.VMEM((ny - 1, half, head), BF16),
        pltpu.VMEM((nz - 1, half, head), BF16),
        dma((6,)),
        dma((nz,)),
        dma((nz,)),
        dma((nz,)),
        dma((sends,)),
        dma((4,)),
        dma((2,)),
        dma((nz,)),
        dma((nz,)),
        dma((4,)),
        dma((ni,)),
        dma((3,)),
        dma((3,)),
        dma((1,)),
        dma((1,)),
    ]

    def in_hbm(x):
        return pltpu.with_memory_space_constraint(x, pltpu.HBM)

    values, summed, anchor_new, momentum_new = pl.pallas_call(
        functools.partial(exchange, nz, ny, ni),
        out_shape=[
            pltpu.VMEM((tall, head), BF16),
            pltpu.VMEM(whole, F32),
            pltpu.VMEM(whole, F32),
            pltpu.VMEM(whole, F32),
        ],
        in_specs=[hbm] * 7,
        out_specs=[vmem] * 4,
        scratch_shapes=scratch,
        compiler_params=pltpu.CompilerParams(
            collective_id=0, has_side_effects=True, vmem_limit_bytes=24 * 2**20
        ),
        name="exchange",
    )(in_hbm(tokens), in_hbm(target), in_hbm(weight), in_hbm(gain), in_hbm(anchor), in_hbm(snapshot), in_hbm(momentum))
    shapes = [(tall, head), shard, line, shard, shard, line, line, whole, whole]
    return pl.pallas_call(
        functools.partial(finish, dim),
        out_shape=[pltpu.HBM(shape, F32 if n else BF16) for n, shape in enumerate(shapes)],
        in_specs=[vmem] * 10,
        out_specs=[hbm] * 9,
        scratch_shapes=[pltpu.VMEM(shape, F32) for shape in shapes[1:7]] + [dma((9,))],
        compiler_params=pltpu.CompilerParams(vmem_limit_bytes=8 * 2**20),
        name="finish",
    )(
        values,
        summed,
        anchor_new,
        momentum_new,
        weight,
        gain,
        first_weight,
        second_weight,
        first_gain,
        second_gain,
    )


def solution(mesh, nz=NZ, ny=NY):
    rows = P(("island", "fsdp"), None)
    shard = P("island", "fsdp", None)
    line = P("island", "fsdp")
    whole = P("fsdp", None)
    return jax.shard_map(
        functools.partial(per_device, nz, ny, mesh.shape["island"]),
        mesh=mesh,
        in_specs=(rows, rows, shard, line, shard, shard, line, line, whole, shard, whole),
        out_specs=(rows, shard, line, shard, shard, line, line, whole, whole),
        check_vma=False,
    )
```

```python
import functools

import jax
import jax.numpy as jnp
from jax import lax
from jax.experimental import pallas as pl
from jax.experimental.pallas import tpu as pltpu
from jax.sharding import PartitionSpec as P

MESH = pl.DeviceIdType.MESH
NZ, NY, NC = 8, 4, 2
F32, BF16 = jnp.float32, jnp.bfloat16


def ring_order(n):
    return sorted(range(1, n), key=lambda d: (min(d, n - d), d))


def spans(links, n):
    late = [links.count(1), sum(k < n // 2 for k in links), len(links)]
    cuts = [1] + sorted({1 + k for k in late})
    return list(zip(cuts[:-1], cuts[1:]))


def adamw(param, grad, first, second):
    first_next = 0.9 * first + 0.1 * grad
    second_next = 0.95 * second + 0.05 * grad * grad
    inner = param - 0.01 * (first_next / (jnp.sqrt(second_next) + 1e-08) + 0.1 * param)
    return inner, first_next, second_next


def eye(n):
    return lax.broadcasted_iota(jnp.int32, (n, n), 0) == lax.broadcasted_iota(jnp.int32, (n, n), 1)


def as_column(row):
    n = row.shape[1]
    return jnp.sum(jnp.where(eye(n), jnp.broadcast_to(row, (n, n)), 0.0), axis=1, keepdims=True)


def as_row(column):
    n = column.shape[0]
    return jnp.sum(jnp.where(eye(n), jnp.broadcast_to(column, (n, n)), 0.0), axis=0, keepdims=True)


def exchange(
    nz,
    ny,
    ni,
    tokens_hbm,
    target_hbm,
    weight_hbm,
    gain_hbm,
    anchor_hbm,
    snapshot_hbm,
    momentum_hbm,
    values_ref,
    summed,
    anchor_new_ref,
    momentum_new_ref,
    tok,
    halves,
    peer,
    target,
    target_t,
    weight,
    anchor,
    snapshot,
    momentum,
    gain_row,
    own,
    eff_a,
    eff_b,
    squares,
    acc,
    other,
    err_t,
    delta,
    part_a,
    part_b,
    recv_a,
    recv_b,
    send_a,
    send_b,
    last_a,
    last_b,
    load_sem,
    tok_sem,
    push_sem,
    peer_sem,
    send_sem,
    pair_sem,
    ya_sem,
    za_sem,
    zb_sem,
    yb_sem,
    delta_sem,
    ra_sem,
    rb_sem,
    la_sem,
    lb_sem,
):
    f = lax.axis_index("fsdp")
    isl = lax.axis_index("island")
    z, y, c = f // (ny * NC), (f // NC) % ny, f % NC
    rows, head = own.shape
    half = rows // 2
    tall = tok.shape[0]
    width = ny * NC * rows
    dim = tok.shape[1]
    up, low = pl.ds(0, half), pl.ds(half, half)
    near_z, near_y = ring_order(nz), ring_order(ny)
    back_z, back_y = near_z[::-1] + [0], near_y[::-1] + [0]
    place_z = {d: n for n, d in enumerate([0] + near_z)}
    hi, lo = y // 2, y % 2
    spans_z = spans([min(d, nz - d) for d in near_z], nz)
    spans_back_z = [(nz - stop, nz - max(start, 1)) for start, stop in spans_z[::-1]]
    spans_back_z[-1] = (spans_back_z[-1][0], nz)
    spans_back_y = [span for span in ((0, 1), (1, ny - 1), (ny - 1, ny)) if span[0] < span[1]]

    def at_z(d):
        return lax.rem(z + d, nz)

    def at_y(d):
        return lax.rem(y + d, ny)

    def to_z(d):
        return {"island": isl, "fsdp": (at_z(d) * ny + y) * NC + c}

    def to_y(d):
        return {"island": isl, "fsdp": (z * ny + at_y(d)) * NC + c}

    sibling = {"island": isl, "fsdp": (z * ny + y) * NC + 1 - c}

    def to_isl(d):
        return {"island": lax.rem(isl + d, ni), "fsdp": f}

    barrier = pltpu.get_barrier_semaphore()
    partners = [to_z(d) for d in near_z[::-1]] + [to_y(d) for d in near_y] + [to_isl(d) for d in range(1, ni)] + [sibling]
    for partner in partners:
        pl.semaphore_signal(barrier, inc=1, device_id=partner, device_id_type=MESH)

    loads = [
        pltpu.make_async_copy(src, dst, load_sem.at[n])
        for n, (src, dst) in enumerate(
            [
                (weight_hbm.at[0], weight),
                (anchor_hbm, anchor),
                (snapshot_hbm.at[0], snapshot),
                (target_hbm, target.at[0]),
                (momentum_hbm, momentum),
                (gain_hbm, gain_row),
            ]
        )
    ]
    loads[5].start()
    loads[0].start()
    for k in range(nz):
        cols = pl.ds(k * width, width)
        pltpu.make_async_copy(tokens_hbm.at[:, cols], tok.at[:, cols], tok_sem.at[k]).start()
    for load in loads[1:5]:
        load.start()

    scale = 1.0 / float(dim) ** 0.5
    loads[5].wait()
    gain = as_column(gain_row[...])
    loads[0].wait()
    own[...] = (gain * weight[...] * scale).astype(BF16)
    eff_a[0, hi, lo] = own[up]
    eff_b[y, 0] = own[low]

    sent = []

    def send(src, dst, sem, device):
        copy = pltpu.make_async_remote_copy(
            src_ref=src,
            dst_ref=dst,
            send_sem=send_sem.at[len(sent)],
            recv_sem=sem,
            device_id=device,
            device_id_type=MESH,
        )
        copy.start()
        sent.append(copy)

    def arrived(ref, sem):
        pltpu.make_async_copy(ref, ref, sem).wait()

    pl.semaphore_wait(barrier, len(partners))

    for d in near_z:
        n = place_z[nz - d]
        send(own.at[low], eff_b.at[y, n], zb_sem.at[n], to_z(d))
    for d in near_y:
        send(own.at[up], eff_a.at[0, hi, lo], ya_sem.at[1 - d % 2], to_y(d))
    for d in near_z:
        send(own.at[up], eff_a.at[nz - d, hi, lo], za_sem.at[nz - d], to_z(d))
    for d in near_y:
        send(own.at[low], eff_b.at[y, 0], yb_sem.at[0], to_y(d))
    loads[3].wait()
    send(target.at[0], target.at[1], pair_sem.at[0], sibling)
    squares[0] = jnp.zeros((8, tall), F32)

    def push(k):
        return pltpu.make_async_remote_copy(
            src_ref=halves.at[k, 1 - c],
            dst_ref=peer.at[k],
            send_sem=push_sem.at[k],
            recv_sem=peer_sem.at[k],
            device_id=sibling,
            device_id_type=MESH,
        )

    def prepare(k, carry):
        cols = pl.ds(pl.multiple_of(k * width, width), width)
        pltpu.make_async_copy(tokens_hbm.at[:, cols], tok.at[:, cols], tok_sem.at[k]).wait()
        turned = tok[:, cols].T
        block = turned.reshape(ny, NC, rows, tall)
        for core in range(NC):
            halves[k, core] = block[:, core]
        push(k).start()
        wide = turned.astype(F32)
        squares[0] += jnp.sum((wide * wide).reshape(width // 8, 8, tall), axis=0)
        return carry

    def pass_low(g):
        start, stop = spans_z[g]
        for n in range(start, stop):
            arrived(eff_b.at[y, n], zb_sem.at[n])
        span = eff_b.at[y, pl.ds(start, stop - start)]
        for d in near_y:
            send(span, span, yb_sem.at[1 + g], to_y(d))

    def pass_up(other_parity):
        if other_parity:
            arrived(eff_a.at[0, :, 1 - lo], ya_sem.at[0])
        else:
            arrived(eff_a.at[0, 1 - hi, lo], ya_sem.at[1])
        for d in near_z:
            if other_parity:
                send(eff_a.at[0, :, 1 - lo], eff_a.at[nz - d, :, 1 - lo], za_sem.at[nz - d], to_z(d))
            else:
                send(eff_a.at[0, 1 - hi, lo], eff_a.at[nz - d, 1 - hi, lo], za_sem.at[nz - d], to_z(d))

    lax.fori_loop(0, nz // 4, prepare, 0)
    pass_low(0)
    lax.fori_loop(nz // 4, nz // 2, prepare, 0)
    pass_up(True)
    for g in range(1, len(spans_z) - 1):
        pass_low(g)
    if ny > 2:
        pass_up(False)
    pass_low(len(spans_z) - 1)
    lax.fori_loop(nz // 2, nz, prepare, 0)

    send(squares.at[0], squares.at[1], pair_sem.at[1], sibling)
    arrived(target.at[1], pair_sem.at[0])
    for n in range(2):
        target_t[n] = target[n].T
    arrived(squares.at[1], pair_sem.at[1])
    rstd = [lax.rsqrt(jnp.sum(squares[n], axis=0, keepdims=True) / float(dim) + 1e-05) for n in range(2)]

    for n, d in enumerate([0] + near_z):
        zb = at_z(d)
        if d:
            arrived(eff_a.at[d], za_sem.at[d])
        for g, (start, stop) in enumerate([(0, 1)] + spans_z):
            if n == start:
                arrived(eff_b.at[pl.ds(0, ny - 1), pl.ds(start, stop - start)], yb_sem.at[g])
        arrived(peer.at[zb], peer_sem.at[zb])
        upper = eff_a[d].reshape(ny, 1, half, head)
        block = jnp.concatenate([upper, eff_b[:, n][:, None]], axis=1).reshape(ny * rows, head)
        for m, side in enumerate((halves[zb, c], peer[zb])):
            partial = lax.dot_general(
                block, side.reshape(ny * rows, tall), (((0,), (0,)), ((), ())), preferred_element_type=F32
            )
            if n:
                acc[m] += partial
            else:
                acc[m] = partial
    for m in range(2):
        send(acc.at[m], other.at[1 - m], pair_sem.at[2 + m], sibling)

    def projected(m):
        return (acc[m] + other[m]) * rstd[m]

    for m in range(2):
        arrived(other.at[1 - m], pair_sem.at[2 + m])
    for m in range(2):
        err_t[m] = ((projected(m) - target_t[m].astype(F32)) * rstd[m]).astype(BF16)

    def product(left, right):
        total = None
        for m, side in enumerate((left, right)):
            term = lax.dot_general(
                side.reshape(-1, tall), err_t[m], (((1,), (1,)), ((), ())), preferred_element_type=F32
            )
            total = term if m == 0 else total + term
        return total.astype(BF16).reshape(-1, half, head)

    def terms_up(g):
        start, stop = spans_back_y[g]
        for n in range(start, stop):
            yb = at_y(back_y[n])
            part_a[:, n] = product(halves[:, c, yb, up], peer[:, yb, up])
        span = pl.ds(start, stop - start)
        for d in near_z[::-1]:
            send(part_a.at[at_z(d), span], recv_a.at[d - 1, span], ra_sem.at[g], to_z(d))

    def terms_low(g):
        start, stop = spans_back_z[g]
        for n in range(start, stop):
            zb = at_z(back_z[n])
            part_b[:, n] = product(halves[zb, c, :, low], peer[zb, :, low])
        span = pl.ds(start, stop - start)
        for d in near_y[::-1]:
            send(part_b.at[at_y(d), span], recv_b.at[d - 1, span], rb_sem.at[g], to_y(d))

    terms_low(0)
    terms_low(1)
    terms_up(0)
    terms_low(2)
    terms_up(1)
    terms_up(2)

    loads[1].wait()
    loads[2].wait()
    delta[isl] = (anchor[...] - snapshot[...]).astype(BF16)
    for d in range(1, ni):
        send(delta.at[isl], delta.at[isl], delta_sem.at[isl], to_isl(d))

    values_ref[...] = projected(0).astype(BF16).T

    kept = {}

    def add_up(g):
        start, stop = spans_back_y[g]
        span = pl.ds(start, stop - start)
        arrived(recv_a.at[:, span], ra_sem.at[g])
        for n in range(start, stop):
            d = back_y[n]
            total = part_a[z, n].astype(F32) + jnp.sum(recv_a[:, n].astype(F32), axis=0)
            if d:
                send_a[n] = total.astype(BF16)
                send(send_a.at[n], last_a.at[d - 1], la_sem.at[0], to_y(d))
            else:
                kept["up"] = total

    def add_low(g):
        start, stop = spans_back_z[g]
        span = pl.ds(start, stop - start)
        arrived(recv_b.at[:, span], rb_sem.at[g])
        for n in range(start, stop):
            d = back_z[n]
            total = part_b[y, n].astype(F32) + jnp.sum(recv_b[:, n].astype(F32), axis=0)
            if d:
                send_b[d - 1] = total.astype(BF16)
                send(send_b.at[d - 1], last_b.at[d - 1], lb_sem.at[0], to_z(d))
            else:
                kept["low"] = total

    for g in range(3):
        if g < len(spans_back_z):
            add_low(g)
        if g < len(spans_back_y) - 1:
            add_up(g)
    add_up(len(spans_back_y) - 1)

    loads[4].wait()
    for d in range(1, ni):
        there = lax.rem(isl + d, ni)
        arrived(delta.at[there], delta_sem.at[there])
    delta_sum = delta[0].astype(F32)
    for n in range(1, ni):
        delta_sum = delta_sum + delta[n].astype(F32)
    mean_delta = delta_sum / float(ni)
    momentum_next = 0.9 * momentum[...] + mean_delta
    anchor_next = anchor[...] - 0.7 * (mean_delta + 0.9 * momentum_next)
    momentum_new_ref[...] = momentum_next
    anchor_new_ref[...] = anchor_next

    arrived(last_a, la_sem.at[0])
    summed[up, :] = kept["up"] + jnp.sum(last_a[...].astype(F32), axis=0)
    arrived(last_b, lb_sem.at[0])
    summed[low, :] = kept["low"] + jnp.sum(last_b[...].astype(F32), axis=0)
    for copy in sent:
        copy.wait_send()
    for k in range(nz):
        push(k).wait_send()


def finish(
    dim,
    values,
    summed,
    anchor_new,
    momentum_new,
    weight,
    gain,
    first_w,
    second_w,
    first_g,
    second_g,
    values_out,
    weight_out,
    gain_out,
    first_w_out,
    second_w_out,
    first_g_out,
    second_g_out,
    anchor_out,
    momentum_out,
    weight_new,
    gain_new,
    first_w_new,
    second_w_new,
    first_g_new,
    second_g_new,
    sem,
):
    scale = 1.0 / float(dim) ** 0.5
    started = []

    def store(src, dst):
        copy = pltpu.make_async_copy(src, dst, sem.at[len(started)])
        copy.start()
        started.append(copy)

    store(values, values_out)
    store(anchor_new, anchor_out)
    store(momentum_new, momentum_out)
    grad = summed[...]
    old = weight[0]
    grad_weight = as_column(gain[...]) * grad * scale
    inner, first_w_new[0], second_w_new[0] = adamw(old, grad_weight, first_w[0], second_w[0])
    weight_new[0] = 0.5 * inner + 0.5 * anchor_new[...]
    store(weight_new, weight_out)
    store(first_w_new, first_w_out)
    store(second_w_new, second_w_out)
    grad_gain = as_row(jnp.sum(old * grad, axis=1, keepdims=True)) * scale
    gain_new[...], first_g_new[...], second_g_new[...] = adamw(gain[...], grad_gain, first_g[...], second_g[...])
    store(gain_new, gain_out)
    store(first_g_new, first_g_out)
    store(second_g_new, second_g_out)
    for copy in started:
        copy.wait()


def per_device(
    nz,
    ny,
    ni,
    tokens,
    target,
    weight,
    gain,
    first_weight,
    second_weight,
    first_gain,
    second_gain,
    anchor,
    snapshot,
    momentum,
):
    tall, dim = tokens.shape
    _, rows, head = weight.shape
    half = rows // 2
    vmem = pl.BlockSpec(memory_space=pltpu.VMEM)
    hbm = pl.BlockSpec(memory_space=pl.ANY)
    shard, line = (1, rows, head), (1, rows)
    whole = (rows, head)
    dma = pltpu.SemaphoreType.DMA
    sends = 4 * (nz - 1) + 5 * (ny - 1) + 4
    sends += 4 * (nz - 1) + 4 * (ny - 1) + (ni - 1)
    scratch = [
        pltpu.VMEM((tall, dim), BF16),
        pltpu.VMEM((nz, NC, ny, rows, tall), BF16),
        pltpu.VMEM((nz, ny, rows, tall), BF16),
        pltpu.VMEM((2, tall, head), BF16),
        pltpu.VMEM((2, head, tall), BF16),
        *[pltpu.VMEM((rows, head), F32) for _ in range(4)],
        pltpu.VMEM(line, F32),
        pltpu.VMEM((rows, head), BF16),
        pltpu.VMEM((nz, ny // 2, 2, half, head), BF16),
        pltpu.VMEM((ny, nz, half, head), BF16),
        pltpu.VMEM((2, 8, tall), F32),
        pltpu.VMEM((2, head, tall), F32),
        pltpu.VMEM((2, head, tall), F32),
        pltpu.VMEM((2, head, tall), BF16),
        pltpu.VMEM((ni, rows, head), BF16),
        pltpu.VMEM((nz, ny, half, head), BF16),
        pltpu.VMEM((ny, nz, half, head), BF16),
        pltpu.VMEM((nz - 1, ny, half, head), BF16),
        pltpu.VMEM((ny - 1, nz, half, head), BF16),
        pltpu.VMEM((ny - 1, half, head), BF16),
        pltpu.VMEM((nz - 1, half, head), BF16),
        pltpu.VMEM((ny - 1, half, head), BF16),
        pltpu.VMEM((nz - 1, half, head), BF16),
        dma((6,)),
        dma((nz,)),
        dma((nz,)),
        dma((nz,)),
        dma((sends,)),
        dma((4,)),
        dma((2,)),
        dma((nz,)),
        dma((nz,)),
        dma((4,)),
        dma((ni,)),
        dma((3,)),
        dma((3,)),
        dma((1,)),
        dma((1,)),
    ]

    def in_hbm(x):
        return pltpu.with_memory_space_constraint(x, pltpu.HBM)

    values, summed, anchor_new, momentum_new = pl.pallas_call(
        functools.partial(exchange, nz, ny, ni),
        out_shape=[
            pltpu.VMEM((tall, head), BF16),
            pltpu.VMEM(whole, F32),
            pltpu.VMEM(whole, F32),
            pltpu.VMEM(whole, F32),
        ],
        in_specs=[hbm] * 7,
        out_specs=[vmem] * 4,
        scratch_shapes=scratch,
        compiler_params=pltpu.CompilerParams(
            collective_id=0, has_side_effects=True, vmem_limit_bytes=24 * 2**20
        ),
        name="exchange",
    )(in_hbm(tokens), in_hbm(target), in_hbm(weight), in_hbm(gain), in_hbm(anchor), in_hbm(snapshot), in_hbm(momentum))
    shapes = [(tall, head), shard, line, shard, shard, line, line, whole, whole]
    return pl.pallas_call(
        functools.partial(finish, dim),
        out_shape=[pltpu.HBM(shape, F32 if n else BF16) for n, shape in enumerate(shapes)],
        in_specs=[vmem] * 10,
        out_specs=[hbm] * 9,
        scratch_shapes=[pltpu.VMEM(shape, F32) for shape in shapes[1:7]] + [dma((9,))],
        compiler_params=pltpu.CompilerParams(vmem_limit_bytes=8 * 2**20),
        name="finish",
    )(
        values,
        summed,
        anchor_new,
        momentum_new,
        weight,
        gain,
        first_weight,
        second_weight,
        first_gain,
        second_gain,
    )


def solution(mesh, nz=NZ, ny=NY):
    rows = P(("island", "fsdp"), None)
    shard = P("island", "fsdp", None)
    line = P("island", "fsdp")
    whole = P("fsdp", None)
    return jax.shard_map(
        functools.partial(per_device, nz, ny, mesh.shape["island"]),
        mesh=mesh,
        in_specs=(rows, rows, shard, line, shard, shard, line, line, whole, shard, whole),
        out_specs=(rows, shard, line, shard, shard, line, line, whole, whole),
        check_vma=False,
    )
```

```python
import functools

import jax
import jax.numpy as jnp
from jax import lax
from jax.experimental import pallas as pl
from jax.experimental.pallas import tpu as pltpu
from jax.sharding import PartitionSpec as P

MESH = pl.DeviceIdType.MESH
NZ, NY, NC = 8, 4, 2
F32, BF16 = jnp.float32, jnp.bfloat16


def ring_order(n):
    return sorted(range(1, n), key=lambda d: (min(d, n - d), d))


def spans(links, n):
    late = [links.count(1), sum(k < n // 2 for k in links), len(links)]
    cuts = [1] + sorted({1 + k for k in late})
    return list(zip(cuts[:-1], cuts[1:]))


def adamw(param, grad, first, second):
    first_next = 0.9 * first + 0.1 * grad
    second_next = 0.95 * second + 0.05 * grad * grad
    inner = param - 0.01 * (first_next / (jnp.sqrt(second_next) + 1e-08) + 0.1 * param)
    return inner, first_next, second_next


def eye(n):
    return lax.broadcasted_iota(jnp.int32, (n, n), 0) == lax.broadcasted_iota(jnp.int32, (n, n), 1)


def as_column(row):
    n = row.shape[1]
    return jnp.sum(jnp.where(eye(n), jnp.broadcast_to(row, (n, n)), 0.0), axis=1, keepdims=True)


def as_row(column):
    n = column.shape[0]
    return jnp.sum(jnp.where(eye(n), jnp.broadcast_to(column, (n, n)), 0.0), axis=0, keepdims=True)


def exchange(
    nz,
    ny,
    ni,
    tokens_hbm,
    target_hbm,
    weight_hbm,
    gain_hbm,
    anchor_hbm,
    snapshot_hbm,
    momentum_hbm,
    values_ref,
    summed,
    anchor_new_ref,
    momentum_new_ref,
    tok,
    halves,
    peer,
    target,
    target_t,
    weight,
    anchor,
    snapshot,
    momentum,
    gain_row,
    own,
    eff_a,
    eff_b,
    squares,
    acc,
    other,
    err_t,
    delta,
    part_a,
    part_b,
    recv_a,
    recv_b,
    send_a,
    send_b,
    last_a,
    last_b,
    load_sem,
    tok_sem,
    push_sem,
    peer_sem,
    send_sem,
    pair_sem,
    ya_sem,
    za_sem,
    zb_sem,
    yb_sem,
    delta_sem,
    ra_sem,
    rb_sem,
    la_sem,
    lb_sem,
):
    f = lax.axis_index("fsdp")
    isl = lax.axis_index("island")
    z, y, c = f // (ny * NC), (f // NC) % ny, f % NC
    rows, head = own.shape
    half = rows // 2
    tall = tok.shape[0]
    width = ny * NC * rows
    dim = tok.shape[1]
    up, low = pl.ds(0, half), pl.ds(half, half)
    near_z, near_y = ring_order(nz), ring_order(ny)
    back_z, back_y = near_z[::-1] + [0], near_y[::-1] + [0]
    place_z = {d: n for n, d in enumerate([0] + near_z)}
    hi, lo = y // 2, y % 2
    spans_z = spans([min(d, nz - d) for d in near_z], nz)
    spans_back_z = [(nz - stop, nz - max(start, 1)) for start, stop in spans_z[::-1]]
    spans_back_z[-1] = (spans_back_z[-1][0], nz)
    spans_back_y = [span for span in ((0, 1), (1, ny - 1), (ny - 1, ny)) if span[0] < span[1]]

    def at_z(d):
        return lax.rem(z + d, nz)

    def at_y(d):
        return lax.rem(y + d, ny)

    def to_z(d):
        return {"island": isl, "fsdp": (at_z(d) * ny + y) * NC + c}

    def to_y(d):
        return {"island": isl, "fsdp": (z * ny + at_y(d)) * NC + c}

    sibling = {"island": isl, "fsdp": (z * ny + y) * NC + 1 - c}

    def to_isl(d):
        return {"island": lax.rem(isl + d, ni), "fsdp": f}

    barrier = pltpu.get_barrier_semaphore()
    partners = [to_z(d) for d in near_z[::-1]] + [to_y(d) for d in near_y] + [to_isl(d) for d in range(1, ni)] + [sibling]
    for partner in partners:
        pl.semaphore_signal(barrier, inc=1, device_id=partner, device_id_type=MESH)

    loads = [
        pltpu.make_async_copy(src, dst, load_sem.at[n])
        for n, (src, dst) in enumerate(
            [
                (weight_hbm.at[0], weight),
                (anchor_hbm, anchor),
                (snapshot_hbm.at[0], snapshot),
                (target_hbm, target.at[0]),
                (momentum_hbm, momentum),
                (gain_hbm, gain_row),
            ]
        )
    ]
    loads[5].start()
    loads[0].start()
    for k in range(nz):
        cols = pl.ds(k * width, width)
        pltpu.make_async_copy(tokens_hbm.at[:, cols], tok.at[:, cols], tok_sem.at[k]).start()
    for load in loads[1:5]:
        load.start()

    scale = 1.0 / float(dim) ** 0.5
    loads[5].wait()
    gain = as_column(gain_row[...])
    loads[0].wait()
    own[...] = (gain * weight[...] * scale).astype(BF16)
    eff_a[0, hi, lo] = own[up]
    eff_b[y, 0] = own[low]

    sent = []

    def send(src, dst, sem, device):
        copy = pltpu.make_async_remote_copy(
            src_ref=src,
            dst_ref=dst,
            send_sem=send_sem.at[len(sent)],
            recv_sem=sem,
            device_id=device,
            device_id_type=MESH,
        )
        copy.start()
        sent.append(copy)

    def arrived(ref, sem):
        pltpu.make_async_copy(ref, ref, sem).wait()

    pl.semaphore_wait(barrier, len(partners))

    for d in near_z:
        n = place_z[nz - d]
        send(own.at[low], eff_b.at[y, n], zb_sem.at[n], to_z(d))
    for d in near_y:
        send(own.at[up], eff_a.at[0, hi, lo], ya_sem.at[1 - d % 2], to_y(d))
    for d in near_z:
        send(own.at[up], eff_a.at[nz - d, hi, lo], za_sem.at[nz - d], to_z(d))
    for d in near_y:
        send(own.at[low], eff_b.at[y, 0], yb_sem.at[0], to_y(d))
    loads[3].wait()
    send(target.at[0], target.at[1], pair_sem.at[0], sibling)
    squares[0] = jnp.zeros((8, tall), F32)

    def push(k):
        return pltpu.make_async_remote_copy(
            src_ref=halves.at[k, 1 - c],
            dst_ref=peer.at[k],
            send_sem=push_sem.at[k],
            recv_sem=peer_sem.at[k],
            device_id=sibling,
            device_id_type=MESH,
        )

    def prepare(k, carry):
        cols = pl.ds(pl.multiple_of(k * width, width), width)
        pltpu.make_async_copy(tokens_hbm.at[:, cols], tok.at[:, cols], tok_sem.at[k]).wait()
        turned = tok[:, cols].T
        block = turned.reshape(ny, NC, rows, tall)
        for core in range(NC):
            halves[k, core] = block[:, core]
        push(k).start()
        wide = turned.astype(F32)
        squares[0] += jnp.sum((wide * wide).reshape(width // 8, 8, tall), axis=0)
        return carry

    def pass_low(g):
        start, stop = spans_z[g]
        for n in range(start, stop):
            arrived(eff_b.at[y, n], zb_sem.at[n])
        span = eff_b.at[y, pl.ds(start, stop - start)]
        for d in near_y:
            send(span, span, yb_sem.at[1 + g], to_y(d))

    def pass_up(other_parity):
        if other_parity:
            arrived(eff_a.at[0, :, 1 - lo], ya_sem.at[0])
        else:
            arrived(eff_a.at[0, 1 - hi, lo], ya_sem.at[1])
        for d in near_z:
            if other_parity:
                send(eff_a.at[0, :, 1 - lo], eff_a.at[nz - d, :, 1 - lo], za_sem.at[nz - d], to_z(d))
            else:
                send(eff_a.at[0, 1 - hi, lo], eff_a.at[nz - d, 1 - hi, lo], za_sem.at[nz - d], to_z(d))

    lax.fori_loop(0, nz // 4, prepare, 0)
    pass_low(0)
    lax.fori_loop(nz // 4, nz // 2, prepare, 0)
    pass_up(True)
    for g in range(1, len(spans_z) - 1):
        pass_low(g)
    if ny > 2:
        pass_up(False)
    pass_low(len(spans_z) - 1)
    lax.fori_loop(nz // 2, nz, prepare, 0)

    send(squares.at[0], squares.at[1], pair_sem.at[1], sibling)
    arrived(target.at[1], pair_sem.at[0])
    for n in range(2):
        target_t[n] = target[n].T
    arrived(squares.at[1], pair_sem.at[1])
    rstd = [lax.rsqrt(jnp.sum(squares[n], axis=0, keepdims=True) / float(dim) + 1e-05) for n in range(2)]

    for n, d in enumerate([0] + near_z):
        zb = at_z(d)
        if d:
            arrived(eff_a.at[d], za_sem.at[d])
        for g, (start, stop) in enumerate([(0, 1)] + spans_z):
            if n == start:
                arrived(eff_b.at[pl.ds(0, ny - 1), pl.ds(start, stop - start)], yb_sem.at[g])
        arrived(peer.at[zb], peer_sem.at[zb])
        upper = eff_a[d].reshape(ny, 1, half, head)
        block = jnp.concatenate([upper, eff_b[:, n][:, None]], axis=1).reshape(ny * rows, head)
        for m in (1, 0):
            side = peer[zb] if m else halves[zb, c]
            partial = lax.dot_general(
                block, side.reshape(ny * rows, tall), (((0,), (0,)), ((), ())), preferred_element_type=F32
            )
            if n:
                acc[m] += partial
            else:
                acc[m] = partial
            if n == nz - 1:
                send(acc.at[m], other.at[1 - m], pair_sem.at[2 + m], sibling)

    def projected(m):
        return (acc[m] + other[m]) * rstd[m]

    for m in range(2):
        arrived(other.at[m], pair_sem.at[3 - m])
        err_t[m] = ((projected(m) - target_t[m].astype(F32)) * rstd[m]).astype(BF16)

    def product(left, right):
        total = None
        for m, side in enumerate((left, right)):
            term = lax.dot_general(
                side.reshape(-1, tall), err_t[m], (((1,), (1,)), ((), ())), preferred_element_type=F32
            )
            total = term if m == 0 else total + term
        return total.astype(BF16).reshape(-1, half, head)

    def terms_up(g):
        start, stop = spans_back_y[g]
        for n in range(start, stop):
            yb = at_y(back_y[n])
            part_a[:, n] = product(halves[:, c, yb, up], peer[:, yb, up])
        span = pl.ds(start, stop - start)
        for d in near_z[::-1]:
            send(part_a.at[at_z(d), span], recv_a.at[d - 1, span], ra_sem.at[g], to_z(d))

    def terms_low(g):
        start, stop = spans_back_z[g]
        for n in range(start, stop):
            zb = at_z(back_z[n])
            part_b[:, n] = product(halves[zb, c, :, low], peer[zb, :, low])
        span = pl.ds(start, stop - start)
        for d in near_y[::-1]:
            send(part_b.at[at_y(d), span], recv_b.at[d - 1, span], rb_sem.at[g], to_y(d))

    terms_low(0)
    terms_low(1)
    terms_up(0)
    terms_low(2)
    terms_up(1)
    terms_up(2)

    loads[1].wait()
    loads[2].wait()
    delta[isl] = (anchor[...] - snapshot[...]).astype(BF16)
    for d in range(1, ni):
        send(delta.at[isl], delta.at[isl], delta_sem.at[isl], to_isl(d))

    values_ref[...] = projected(0).astype(BF16).T

    kept = {}

    def add_up(g):
        start, stop = spans_back_y[g]
        span = pl.ds(start, stop - start)
        arrived(recv_a.at[:, span], ra_sem.at[g])
        for n in range(start, stop):
            d = back_y[n]
            total = part_a[z, n].astype(F32) + jnp.sum(recv_a[:, n].astype(F32), axis=0)
            if d:
                send_a[n] = total.astype(BF16)
                send(send_a.at[n], last_a.at[d - 1], la_sem.at[0], to_y(d))
            else:
                kept["up"] = total

    def add_low(g):
        start, stop = spans_back_z[g]
        span = pl.ds(start, stop - start)
        arrived(recv_b.at[:, span], rb_sem.at[g])
        for n in range(start, stop):
            d = back_z[n]
            total = part_b[y, n].astype(F32) + jnp.sum(recv_b[:, n].astype(F32), axis=0)
            if d:
                send_b[d - 1] = total.astype(BF16)
                send(send_b.at[d - 1], last_b.at[d - 1], lb_sem.at[0], to_z(d))
            else:
                kept["low"] = total

    for g in range(3):
        if g < len(spans_back_z):
            add_low(g)
        if g < len(spans_back_y) - 1:
            add_up(g)
    add_up(len(spans_back_y) - 1)

    loads[4].wait()
    for d in range(1, ni):
        there = lax.rem(isl + d, ni)
        arrived(delta.at[there], delta_sem.at[there])
    delta_sum = delta[0].astype(F32)
    for n in range(1, ni):
        delta_sum = delta_sum + delta[n].astype(F32)
    mean_delta = delta_sum / float(ni)
    momentum_next = 0.9 * momentum[...] + mean_delta
    anchor_next = anchor[...] - 0.7 * (mean_delta + 0.9 * momentum_next)
    momentum_new_ref[...] = momentum_next
    anchor_new_ref[...] = anchor_next

    arrived(last_a, la_sem.at[0])
    summed[up, :] = kept["up"] + jnp.sum(last_a[...].astype(F32), axis=0)
    arrived(last_b, lb_sem.at[0])
    summed[low, :] = kept["low"] + jnp.sum(last_b[...].astype(F32), axis=0)
    for copy in sent:
        copy.wait_send()
    for k in range(nz):
        push(k).wait_send()


def finish(
    dim,
    values,
    summed,
    anchor_new,
    momentum_new,
    weight,
    gain,
    first_w,
    second_w,
    first_g,
    second_g,
    values_out,
    weight_out,
    gain_out,
    first_w_out,
    second_w_out,
    first_g_out,
    second_g_out,
    anchor_out,
    momentum_out,
    weight_new,
    gain_new,
    first_w_new,
    second_w_new,
    first_g_new,
    second_g_new,
    sem,
):
    scale = 1.0 / float(dim) ** 0.5
    started = []

    def store(src, dst):
        copy = pltpu.make_async_copy(src, dst, sem.at[len(started)])
        copy.start()
        started.append(copy)

    store(values, values_out)
    store(anchor_new, anchor_out)
    store(momentum_new, momentum_out)
    grad = summed[...]
    old = weight[0]
    grad_weight = as_column(gain[...]) * grad * scale
    inner, first_w_new[0], second_w_new[0] = adamw(old, grad_weight, first_w[0], second_w[0])
    weight_new[0] = 0.5 * inner + 0.5 * anchor_new[...]
    store(weight_new, weight_out)
    store(first_w_new, first_w_out)
    store(second_w_new, second_w_out)
    grad_gain = as_row(jnp.sum(old * grad, axis=1, keepdims=True)) * scale
    gain_new[...], first_g_new[...], second_g_new[...] = adamw(gain[...], grad_gain, first_g[...], second_g[...])
    store(gain_new, gain_out)
    store(first_g_new, first_g_out)
    store(second_g_new, second_g_out)
    for copy in started:
        copy.wait()


def per_device(
    nz,
    ny,
    ni,
    tokens,
    target,
    weight,
    gain,
    first_weight,
    second_weight,
    first_gain,
    second_gain,
    anchor,
    snapshot,
    momentum,
):
    tall, dim = tokens.shape
    _, rows, head = weight.shape
    half = rows // 2
    vmem = pl.BlockSpec(memory_space=pltpu.VMEM)
    hbm = pl.BlockSpec(memory_space=pl.ANY)
    shard, line = (1, rows, head), (1, rows)
    whole = (rows, head)
    dma = pltpu.SemaphoreType.DMA
    sends = 4 * (nz - 1) + 5 * (ny - 1) + 4
    sends += 4 * (nz - 1) + 4 * (ny - 1) + (ni - 1)
    scratch = [
        pltpu.VMEM((tall, dim), BF16),
        pltpu.VMEM((nz, NC, ny, rows, tall), BF16),
        pltpu.VMEM((nz, ny, rows, tall), BF16),
        pltpu.VMEM((2, tall, head), BF16),
        pltpu.VMEM((2, head, tall), BF16),
        *[pltpu.VMEM((rows, head), F32) for _ in range(4)],
        pltpu.VMEM(line, F32),
        pltpu.VMEM((rows, head), BF16),
        pltpu.VMEM((nz, ny // 2, 2, half, head), BF16),
        pltpu.VMEM((ny, nz, half, head), BF16),
        pltpu.VMEM((2, 8, tall), F32),
        pltpu.VMEM((2, head, tall), F32),
        pltpu.VMEM((2, head, tall), F32),
        pltpu.VMEM((2, head, tall), BF16),
        pltpu.VMEM((ni, rows, head), BF16),
        pltpu.VMEM((nz, ny, half, head), BF16),
        pltpu.VMEM((ny, nz, half, head), BF16),
        pltpu.VMEM((nz - 1, ny, half, head), BF16),
        pltpu.VMEM((ny - 1, nz, half, head), BF16),
        pltpu.VMEM((ny - 1, half, head), BF16),
        pltpu.VMEM((nz - 1, half, head), BF16),
        pltpu.VMEM((ny - 1, half, head), BF16),
        pltpu.VMEM((nz - 1, half, head), BF16),
        dma((6,)),
        dma((nz,)),
        dma((nz,)),
        dma((nz,)),
        dma((sends,)),
        dma((4,)),
        dma((2,)),
        dma((nz,)),
        dma((nz,)),
        dma((4,)),
        dma((ni,)),
        dma((3,)),
        dma((3,)),
        dma((1,)),
        dma((1,)),
    ]

    def in_hbm(x):
        return pltpu.with_memory_space_constraint(x, pltpu.HBM)

    values, summed, anchor_new, momentum_new = pl.pallas_call(
        functools.partial(exchange, nz, ny, ni),
        out_shape=[
            pltpu.VMEM((tall, head), BF16),
            pltpu.VMEM(whole, F32),
            pltpu.VMEM(whole, F32),
            pltpu.VMEM(whole, F32),
        ],
        in_specs=[hbm] * 7,
        out_specs=[vmem] * 4,
        scratch_shapes=scratch,
        compiler_params=pltpu.CompilerParams(
            collective_id=0, has_side_effects=True, vmem_limit_bytes=24 * 2**20
        ),
        name="exchange",
    )(in_hbm(tokens), in_hbm(target), in_hbm(weight), in_hbm(gain), in_hbm(anchor), in_hbm(snapshot), in_hbm(momentum))
    shapes = [(tall, head), shard, line, shard, shard, line, line, whole, whole]
    return pl.pallas_call(
        functools.partial(finish, dim),
        out_shape=[pltpu.HBM(shape, F32 if n else BF16) for n, shape in enumerate(shapes)],
        in_specs=[vmem] * 10,
        out_specs=[hbm] * 9,
        scratch_shapes=[pltpu.VMEM(shape, F32) for shape in shapes[1:7]] + [dma((9,))],
        compiler_params=pltpu.CompilerParams(vmem_limit_bytes=8 * 2**20),
        name="finish",
    )(
        values,
        summed,
        anchor_new,
        momentum_new,
        weight,
        gain,
        first_weight,
        second_weight,
        first_gain,
        second_gain,
    )


def solution(mesh, nz=NZ, ny=NY):
    rows = P(("island", "fsdp"), None)
    shard = P("island", "fsdp", None)
    line = P("island", "fsdp")
    whole = P("fsdp", None)
    return jax.shard_map(
        functools.partial(per_device, nz, ny, mesh.shape["island"]),
        mesh=mesh,
        in_specs=(rows, rows, shard, line, shard, shard, line, line, whole, shard, whole),
        out_specs=(rows, shard, line, shard, shard, line, line, whole, whole),
        check_vma=False,
    )
```
